32 devices in a mesh: gx: 8 (over z, core), gy: 4 (over y, x).
Axes of the slice: x: 2, y: 2, z: 4, core: 2. Of those that a mesh axis runs over, the one named last changes fastest.
Arguments:
- velocity: float32 [3, 256, 256, 128], P(None, 'gx', 'gy'), may hold values from -6 to 6
- stress: float32 [6, 256, 256, 128], P(None, 'gx', 'gy'), may hold values from -9 to 9
- material: float32 [3, 256, 256, 128], P(None, 'gx', 'gy'), may hold values from 0.3 to 1
- src_x: int32 [2, 64], replicated, may hold values from 0 to 255
- src_y: int32 [2, 64], replicated, may hold values from 0 to 255
- src_amp: float32 [2, 64], replicated, may hold values from -30 to 30
- chan_block: int32 [8192, 1], P(('gx', 'gy')), may hold values from 0 to 31; in each aligned block of 256 rows (0 to 255, 256 to 511, ...) at most 16 rows name the same one
- chan_cell: int32 [8192], P(('gx', 'gy')), may hold values from 0 to 262143
- chan_azimuth: float32 [8192], P(('gx', 'gy')), may hold values from -3.140625 to 3.140625
- gauge: int32 [8192], P(('gx', 'gy')), may hold values from 2 to 16
Outputs:
- velocity_out: float32 [3, 256, 256, 128], P(None, 'gx', 'gy')
- stress_out: float32 [6, 256, 256, 128], P(None, 'gx', 'gy')
- strain_rate: float32 [8192], P(('gx', 'gy'))
The draws below stay inside these ranges and needn't reach their ends.
Inputs may be any that keep to these rules, and one draw needn't show every extreme that they name: `chan_block`: among the 256 channels of one fibre segment (the channels of one device) no grid block is named more than 16 times, and in every draw some grid block is named exactly 16 times by some segment.
All inputs are finite; a program needn't handle non-finite values.
Results may differ from the reference program's by a relative error of at most 0.00012.
Values sent between devices are 32-bit elements; how exact they have to be, the bound alone decides.
A program may use at most 128 MiB of HBM per device.

```python
import math
import jax
import jax.numpy as jnp
import numpy as np
from jax import lax

CX = 32
CY = 64
NZ = 128
STEPS = 2
NSRC = 64
CH_DEV = 256
NX = 256
NY = 256
CH = 8192
CAP = 16
N_GX = 8
N_GY = 4


def draw_stress(key, part):
    rough_key = jax.random.fold_in(key, 11)
    count_key = jax.random.fold_in(key, 12)
    sign_key = jax.random.fold_in(key, 13)
    phase_key = jax.random.fold_in(key, 14)
    rough = jnp.clip(jax.random.normal(rough_key, (6, NX, NY, NZ), jnp.float32), -5.0, 5.0)
    height = 4.0
    counts = jax.random.randint(count_key, (6, 3), 7, 12)
    signs = jax.random.randint(sign_key, (6, 3), 0, 2) * 2 - 1
    waves = (counts * signs).astype(jnp.int32)
    phases = jax.random.uniform(phase_key, (6,), jnp.float32, 0.0, 2.0 * math.pi)
    pos_x = jnp.arange(NX, dtype=jnp.int32)
    pos_y = jnp.arange(NY, dtype=jnp.int32)
    pos_z = jnp.arange(NZ, dtype=jnp.int32)
    index = (waves[:, 0, None, None, None] * pos_x[None, :, None, None] + waves[:, 1, None, None, None] * pos_y[None, None, :, None] + waves[:, 2, None, None, None] * pos_z[None, None, None, :]) % 128
    angle = index.astype(jnp.float32) * (2.0 * math.pi / 128.0) + phases[:, None, None, None]
    return rough + height * jnp.cos(angle)


def plant(drawn, own_key, smallest, high):
    spot = [jax.random.randint(jax.random.fold_in(own_key, axis), (), 0, length) for axis, length in enumerate(drawn.shape)]
    widest = drawn.shape.index(max(drawn.shape))
    beside = spot[:widest] + [(spot[widest] + 1) % drawn.shape[widest]] + spot[widest + 1:]
    return drawn.at[tuple(spot)].set(smallest).at[tuple(beside)].set(high)


def levels(own_key, shape, shards, least, top_value):
    factor_of, own = 1.0, jax.random.fold_in(own_key, 6)
    for position, shards_of in shards:
        heights = jnp.exp(jax.random.uniform(jax.random.fold_in(own, position), (shards_of,), jnp.float32, least / len(shards), top_value / len(shards)))
        factor_of = factor_of * jnp.repeat(heights, shape[position] // shards_of).reshape([-1 if axis == position else 1 for axis in range(len(shape))])
    return factor_of


def shared_out(rng, own, number, rows, count, top, limit, lean):
    ranking = jax.random.permutation(rng, count)
    heavy_load, ordinary = load_shares(count, rows * top, limit, lean, True), load_shares(count, rows * top, limit, lean, False)
    places = jnp.arange(count)

    def named(sizes, turn):
        used = int((sizes > 0).sum())
        fixed = max(1, used // 4)
        passed = fixed + (places - fixed + turn * (used - fixed)) % max(1, count - fixed)
        return jnp.zeros((count,), jnp.int32).at[ranking[jnp.where(places < fixed, places, passed)]].set(jnp.asarray(sizes, jnp.int32))

    sizes = jnp.where(number % 4 == 0, named(heavy_load, number // 4), named(ordinary, number - number // 4 - 1))
    mixed = jax.random.permutation(jax.random.fold_in(own, 3), count)
    donor, taker = mixed[0:count // 2 * 2:2], mixed[1:count // 2 * 2:2]
    slack = jnp.minimum(sizes[donor] - 1, limit - sizes[taker]) // 2
    slack = jnp.where((donor == ranking[0]) | (taker == ranking[0]) | (sizes[taker] == 0), 0, jnp.maximum(slack, 0))
    passed = jax.random.randint(jax.random.fold_in(own, 4), (count // 2,), 0, 1 << 20) % (slack + 1)
    sizes = sizes.at[donor].add(-passed).at[taker].add(passed)
    labels = jnp.searchsorted(jnp.cumsum(sizes), jnp.arange(rows * top), side="right").astype(jnp.int32)
    table = labels.reshape(top, rows).T
    table = table[jax.random.permutation(jax.random.fold_in(own, 1), rows)]
    turn = jax.random.randint(jax.random.fold_in(own, 2), (rows, 1), 0, top)
    return jnp.take_along_axis(table, (jnp.arange(top)[None, :] + turn) % top, axis=1)


def load_shares(number_of, total, limit, lean, full):
    loads = [(1 << 20) // math.isqrt(grade ** lean) + 1 for grade in range(1, number_of + 1)]
    largest = limit if full else min(limit, max(-(-total // number_of), total * loads[0] // sum(loads)))
    least = 1 if total - largest >= number_of - 1 else 0
    given, rest = [largest] + [least] * (number_of - 1), total - largest - least * (number_of - 1)
    while rest > 0:
        candidates = [i for i in range(1, number_of) if given[i] < largest] or [i for i in range(1, number_of) if given[i] < limit]
        pool, left = sum([loads[i] for i in candidates]), rest
        for i in candidates:
            addition = min(limit - given[i], max(1, left * loads[i] // pool), rest)
            given[i] = given[i] + addition
            rest = rest - addition
    return np.array(given)


def normal_values(key, dims, width, reach, split=(), held_as=jnp.bfloat16):
    entries = width * jax.random.normal(key, dims, jnp.float32)
    if split:
        entries = entries * levels(key, dims, split, -0.22, 0.18)
    return jnp.clip(entries, -reach, reach).astype(held_as)


def setup_inputs(seed: int = 0) -> dict:
    key_list = jax.random.split(jax.random.key(seed), 11)
    velocity = normal_values(key_list[0], (3, NX, NY, NZ), 1.0, 6.0, ((1, 8), (2, 4)), jnp.float32)
    stress = draw_stress(jax.random.fold_in(key_list[10], 71), 0)
    material = jnp.clip(jnp.exp(math.log(1.0) - 1.2039728 * jax.random.uniform(key_list[2], (3, NX, NY, NZ), jnp.float32) ** levels(key_list[2], (3, NX, NY, NZ), ((1, 8), (2, 4)), -0.2, 0.2)), 0.3, 1.0)
    src_x = plant(jax.random.randint(key_list[3], (STEPS, NSRC), 0, NX), jax.random.fold_in(key_list[3], 1), 0, NX - 1).astype(jnp.int32)
    src_y = plant(jax.random.randint(key_list[4], (STEPS, NSRC), 0, NY), jax.random.fold_in(key_list[4], 1), 0, NY - 1).astype(jnp.int32)
    src_amp = normal_values(key_list[5], (STEPS, NSRC), 5.0, 30.0, (), jnp.float32)
    chan_block_keys = jax.random.split(jax.random.fold_in(key_list[6], 1), CH // CH_DEV)
    chan_block_turns = jax.random.permutation(jax.random.fold_in(key_list[6], 3), CH // CH_DEV)
    chan_block = jax.vmap(lambda own, number: shared_out(jax.random.fold_in(key_list[6], 2), own, number, CH_DEV, N_GX * N_GY, 1, CAP, 2))(chan_block_keys, chan_block_turns).reshape((CH, 1))
    chan_cell = plant(jax.random.randint(key_list[7], (CH,), 0, CX * CY * NZ), jax.random.fold_in(key_list[7], 1), 0, (CX * CY * NZ) - 1).astype(jnp.int32)
    chan_azimuth = jnp.clip(jax.random.uniform(key_list[8], (CH,), jnp.float32, -3.140625, 3.140625), -3.140625, 3.140625)
    gauge = plant(jax.random.randint(key_list[9], (CH,), 2, 17), jax.random.fold_in(key_list[9], 1), 2, 16).astype(jnp.int32)
    return {"velocity": velocity, "stress": stress, "material": material, "src_x": src_x, "src_y": src_y, "src_amp": src_amp, "chan_block": chan_block, "chan_cell": chan_cell, "chan_azimuth": chan_azimuth, "gauge": gauge}


COEFFS = (1225.0 / 1024.0, -245.0 / 3072.0, 49.0 / 5120.0, -5.0 / 7168.0)
time_step = 0.2


def padded(field, axis):
    widths = [(0, 0)] * field.ndim
    widths[axis] = (4, 4)
    return jnp.pad(field, widths)


def forward_diff(extended, axis, length):
    total = 0.0
    for order in range(1, 5):
        ahead = lax.slice_in_dim(extended, 4 + order, 4 + order + length, axis=axis)
        behind = lax.slice_in_dim(extended, 5 - order, 5 - order + length, axis=axis)
        total = total + COEFFS[order - 1] * (ahead - behind)
    return total


def backward_diff(extended, axis, length):
    total = 0.0
    for order in range(1, 5):
        ahead = lax.slice_in_dim(extended, 3 + order, 3 + order + length, axis=axis)
        behind = lax.slice_in_dim(extended, 4 - order, 4 - order + length, axis=axis)
        total = total + COEFFS[order - 1] * (ahead - behind)
    return total


def update_velocity(velocity, stress, buoyancy, force, x_ext, y_ext):
    count_x, count_y, depth = buoyancy.shape
    rate_x = forward_diff(x_ext[0], 0, count_x) + backward_diff(y_ext[0], 1, count_y) + backward_diff(padded(stress[1], 2), 2, depth)
    rate_y = backward_diff(x_ext[2], 0, count_x) + forward_diff(y_ext[2], 1, count_y) + backward_diff(padded(stress[3], 2), 2, depth)
    rate_z = backward_diff(x_ext[1], 0, count_x) + backward_diff(y_ext[1], 1, count_y) + forward_diff(padded(stress[5], 2), 2, depth)
    rate_z = rate_z.at[:, :, 0].add(force)
    return jnp.stack([velocity[0] + time_step * buoyancy * rate_x,
                      velocity[1] + time_step * buoyancy * rate_y,
                      velocity[2] + time_step * buoyancy * rate_z])


def update_stress(velocity, stress, lame, shear, vel_x_ext, vel_y_ext):
    count_x, count_y, depth = lame.shape
    strain_xx = backward_diff(vel_x_ext[0], 0, count_x)
    strain_yy = backward_diff(vel_y_ext[1], 1, count_y)
    strain_zz = backward_diff(padded(velocity[2], 2), 2, depth)
    trace_sum = strain_xx + strain_yy + strain_zz
    shear_xy = forward_diff(vel_y_ext[0], 1, count_y) + forward_diff(vel_x_ext[1], 0, count_x)
    shear_xz = forward_diff(padded(velocity[0], 2), 2, depth) + forward_diff(vel_x_ext[2], 0, count_x)
    shear_yz = forward_diff(padded(velocity[1], 2), 2, depth) + forward_diff(vel_y_ext[2], 1, count_y)
    return jnp.stack([stress[0] + time_step * (lame * trace_sum + 2.0 * shear * strain_xx),
                      stress[1] + time_step * shear * shear_xz,
                      stress[2] + time_step * shear * shear_xy,
                      stress[3] + time_step * shear * shear_yz,
                      stress[4] + time_step * (lame * trace_sum + 2.0 * shear * strain_yy),
                      stress[5] + time_step * (lame * trace_sum + 2.0 * shear * strain_zz)])


def reference(velocity, stress, material, src_x, src_y, src_amp, chan_block, chan_cell, chan_azimuth, gauge):
    lame, shear, buoyancy = material[0], material[1], material[2]
    for step in range(STEPS):
        force = jnp.zeros((NX, NY), jnp.float32).at[src_x[step], src_y[step]].add(src_amp[step])
        velocity = update_velocity(velocity, stress, buoyancy, force, padded(stress[0:3], 1), padded(stress[2:5], 2))
        stress = update_stress(velocity, stress, lame, shear, padded(velocity, 1), padded(velocity, 2))
    block = chan_block[:, 0]
    cell_x = (block // N_GY) * CX + chan_cell // (CY * NZ)
    cell_y = (block % N_GY) * CY + (chan_cell // NZ) % CY
    cell_z = chan_cell % NZ
    along = jnp.cos(chan_azimuth) * velocity[0][cell_x, cell_y, cell_z] + jnp.sin(chan_azimuth) * velocity[1][cell_x, cell_y, cell_z]
    joined = jnp.concatenate([along, jnp.zeros_like(along)])
    positions = jnp.arange(CH, dtype=jnp.int32) + gauge.astype(jnp.int32)
    ahead = jnp.take(joined, positions)
    strain = (ahead - along) / gauge.astype(jnp.float32)
    return velocity, stress, strain
```

```python
import functools

import jax
import jax.numpy as jnp
import ml_dtypes
import numpy as np
from jax import lax
from jax.experimental import pallas as pl
from jax.experimental.pallas import tpu as pltpu
from jax.sharding import PartitionSpec as P

STEPS = 2
COEFFS = (1225.0 / 1024.0, -245.0 / 3072.0, 49.0 / 5120.0, -5.0 / 7168.0)
DT = 0.2
W = 4
PAD = 8
PLANES = 4
MESH = pl.DeviceIdType.MESH


def depth_weights(depth):
    out = np.zeros((2, 2 * depth, 2 * depth), np.float32)
    for which, shift in ((0, 0), (1, -1)):
        table = np.zeros((depth, depth), np.float64)
        for target in range(depth):
            for order in range(1, 5):
                for source, sign in ((target + shift + order, 1.0), (target + shift + 1 - order, -1.0)):
                    if 0 <= source < depth:
                        table[source, target] += sign * COEFFS[order - 1]
        hi = table.astype(np.float32).astype(ml_dtypes.bfloat16).astype(np.float32)
        lo = (table - hi).astype(np.float32)
        out[which, :depth, :depth] = hi
        out[which, :depth, depth:] = lo
        out[which, depth:, :depth] = hi
    return out.astype(ml_dtypes.bfloat16)


def depth_product(values, weights):
    depth = values.shape[1]
    hi = values.astype(jnp.bfloat16)
    lo = (values - hi.astype(jnp.float32)).astype(jnp.bfloat16)
    both = jnp.concatenate([hi, lo], axis=1)
    out = jnp.dot(both, weights, preferred_element_type=jnp.float32)
    return out[:, :depth] + out[:, depth:]


def weighted(load, forward):
    total = None
    shift = 0 if forward else -1
    for order in range(1, 5):
        term = COEFFS[order - 1] * (load(shift + order) - load(shift + 1 - order))
        total = term if total is None else total + term
    return total


def diff_x(ref, f, x, r0, nr, forward):
    return weighted(lambda k: ref[f, x + (W + k), PAD + r0 : PAD + r0 + nr, :], forward)


def diff_y(ref, f, x, r0, nr, forward):
    return weighted(lambda k: ref[f, x + W, PAD + r0 + k : PAD + r0 + k + nr, :], forward)


def own(ref, f, x, r0, nr):
    return ref[f, x + W, PAD + r0 : PAD + r0 + nr, :]


def stress_parts(v, z_of, x, r0, nr, lam, mu):
    exx = diff_x(v, 0, x, r0, nr, False)
    eyy = diff_y(v, 1, x, r0, nr, False)
    ezz = z_of(0)
    common = (DT * lam) * (exx + eyy + ezz)
    dmu = DT * mu
    dmu2 = 2.0 * dmu
    return (
        common + dmu2 * exx,
        dmu * (z_of(1) + diff_x(v, 2, x, r0, nr, True)),
        dmu * (diff_y(v, 0, x, r0, nr, True) + diff_x(v, 1, x, r0, nr, True)),
        dmu * (z_of(2) + diff_y(v, 2, x, r0, nr, True)),
        common + dmu2 * eyy,
        common + dmu2 * ezz,
    )


def main_kernel(
    sizes, cap, stress, velocity, material, weights, force, incoming,
    s1_out, v2_out, picked_out,
    s0, s1, v0, v1, v2, mat, zs, picks, load_sem, send_sem, recv_sem, out_sem,
):
    nx, ny, depth = sizes
    gx, gy = lax.axis_index("gx"), lax.axis_index("gy")
    last_x, last_y = lax.axis_size("gx") - 1, lax.axis_size("gy") - 1
    sides = (
        (gx > 0, "gx", gx - 1),
        (gx < last_x, "gx", gx + 1),
        (gy > 0, "gy", gy - 1),
        (gy < last_y, "gy", gy + 1),
    )
    fields_of = {"s": ((0, 3), (2, 5)), "v": ((0, 3), (0, 3))}
    rows = (slice(PAD, PAD + ny),)[0]
    planes = slice(W, W + nx)

    loads = [
        pltpu.make_async_copy(stress, s0.at[:, planes, rows, :], load_sem.at[0]),
        pltpu.make_async_copy(velocity, v0, load_sem.at[1]),
        pltpu.make_async_copy(material, mat, load_sem.at[2]),
    ]
    for copy in loads:
        copy.start()

    for ref, kind in ((s0, "s"), (s1, "s"), (v1, "v"), (v2, "v")):
        (xa, xb), (ya, yb) = fields_of[kind]

        @pl.when(gx == 0)
        def _():
            ref[xa:xb, 0:W] = jnp.zeros((xb - xa, W, ny + 2 * PAD, depth), jnp.float32)

        @pl.when(gx == last_x)
        def _():
            ref[xa:xb, W + nx :] = jnp.zeros((xb - xa, W, ny + 2 * PAD, depth), jnp.float32)

        @pl.when(gy == 0)
        def _():
            @pl.loop(0, nx)
            def _(x):
                ref[ya:yb, x + W, 0:PAD] = jnp.zeros((yb - ya, PAD, depth), jnp.float32)

        @pl.when(gy == last_y)
        def _():
            @pl.loop(0, nx)
            def _(x):
                ref[ya:yb, x + W, PAD + ny :] = jnp.zeros((yb - ya, PAD, depth), jnp.float32)

    barrier = pltpu.get_barrier_semaphore()
    for exists, axis, other in sides:
        @pl.when(exists)
        def _():
            pl.semaphore_signal(barrier, inc=1, device_id={axis: other}, device_id_type=MESH)
    count = sum(exists.astype(jnp.int32) for exists, _, _ in sides)
    pl.semaphore_wait(barrier, count)

    def transfer(phase, kind, source, target, side, from_input):
        (xa, xb), (ya, yb) = fields_of[kind]
        ox, oy = (0, 0) if from_input else (W, PAD)
        all_x, all_y = slice(ox, ox + nx), slice(oy, oy + ny)
        if side == 0:
            src = source.at[xa:xb, ox : ox + W, all_y, :]
            dst = target.at[xa:xb, W + nx : 2 * W + nx, rows, :]
        elif side == 1:
            src = source.at[xa:xb, ox + nx - W : ox + nx, all_y, :]
            dst = target.at[xa:xb, 0:W, rows, :]
        elif side == 2:
            src = source.at[ya:yb, all_x, oy : oy + W, :]
            dst = target.at[ya:yb, planes, PAD + ny : PAD + ny + W, :]
        else:
            src = source.at[ya:yb, all_x, oy + ny - W : oy + ny, :]
            dst = target.at[ya:yb, planes, PAD - W : PAD, :]
        return pltpu.make_async_remote_copy(
            src_ref=src, dst_ref=dst,
            send_sem=send_sem.at[phase, side], recv_sem=recv_sem.at[phase, side],
            device_id={sides[side][1]: sides[side][2]}, device_id_type=MESH,
        )

    plan = (("s", stress, s0, True), ("v", v1, v1, False), ("s", s1, s1, False), ("v", v2, v2, False))

    def send(phase, which):
        kind, source, target, from_input = plan[phase]
        for side in which:
            @pl.when(sides[side][0])
            def _():
                transfer(phase, kind, source, target, side, from_input).start()

    def arrive(phase):
        kind, source, target, from_input = plan[phase]
        for side in range(4):
            @pl.when(sides[side ^ 1][0])
            def _():
                transfer(phase, kind, source, target, side, from_input).wait_recv()

    def sent(phase):
        kind, source, target, from_input = plan[phase]
        for side in range(4):
            @pl.when(sides[side][0])
            def _():
                transfer(phase, kind, source, target, side, from_input).wait_send()

    def depth_pass(ref, jobs):
        @pl.loop(0, nx // PLANES)
        def _(i):
            x = i * PLANES
            for slot, (f, forward) in enumerate(jobs):
                block = ref[f, pl.ds(x + W, PLANES), PAD : PAD + ny, :].reshape(PLANES * ny, depth)
                out = depth_product(block, weights[0 if forward else 1])
                zs[slot, pl.ds(x, PLANES)] = out.reshape(PLANES, ny, depth)

    def velocity_plane(step, s, x, r0, nr):
        old = (lambda f: v0[f, x, r0 : r0 + nr, :]) if step == 0 else (lambda f: own(v1, f, x, r0, nr))
        new = v1 if step == 0 else v2
        z = lambda k: zs[k, x, r0 : r0 + nr, :]
        db = DT * mat[2, x, r0 : r0 + nr, :]

        def put(f, value):
            updated = old(f) + db * value
            new[f, x + W, PAD + r0 : PAD + r0 + nr, :] = updated
            if step == 1 and f < 2:
                v0[f, x, r0 : r0 + nr, :] = updated

        put(0, diff_x(s, 0, x, r0, nr, True) + diff_y(s, 2, x, r0, nr, False) + z(0))
        put(1, diff_x(s, 2, x, r0, nr, False) + diff_y(s, 4, x, r0, nr, True) + z(1))
        load = pltpu.roll(force[step, r0 : r0 + nr, :], depth - x, 1)
        lane = lax.broadcasted_iota(jnp.int32, (nr, depth), 1)
        rate = diff_x(s, 1, x, r0, nr, False) + diff_y(s, 3, x, r0, nr, False) + z(2)
        put(2, rate + jnp.where(lane == 0, load, 0.0))

    def stress_plane(x, r0, nr):
        lam, mu = mat[0, x, r0 : r0 + nr, :], mat[1, x, r0 : r0 + nr, :]
        z = lambda k: zs[k, x, r0 : r0 + nr, :]
        for f, change in enumerate(stress_parts(v1, z, x, r0, nr, lam, mu)):
            s1[f, x + W, PAD + r0 : PAD + r0 + nr, :] = own(s0, f, x, r0, nr) + change

    def interior(update):
        @pl.loop(W, nx - W)
        def _(x):
            update(x, 8, ny - 16)

    def edges_y(update):
        @pl.loop(0, nx)
        def _(x):
            update(x, 0, 8)
            update(x, ny - 8, 8)

    def edges_x(update):
        @pl.loop(0, 2 * W)
        def _(i):
            update(jnp.where(i < W, i, i + nx - 2 * W), 8, ny - 16)

    def update_of(phase):
        if phase == 1:
            return stress_plane
        return functools.partial(velocity_plane, phase // 2, s0 if phase == 0 else s1)

    v_jobs = ((1, False), (3, False), (5, True))
    s_jobs = ((2, False), (0, True), (1, True))
    send(0, (2, 3, 0, 1))
    loads[0].wait()
    for phase, (ref, jobs) in enumerate(((s0, v_jobs), (v1, s_jobs), (s1, v_jobs))):
        update = update_of(phase)
        depth_pass(ref, jobs)
        if phase == 0:
            loads[1].wait()
            loads[2].wait()
        interior(update)
        arrive(phase)
        edges_y(update)
        send(phase + 1, (2, 3))
        edges_x(update)
        send(phase + 1, (0, 1))
        if phase == 1:
            s1_copy = pltpu.make_async_copy(s1.at[:, planes, rows, :], s1_out, out_sem.at[0])
            s1_copy.start()

    total = incoming.shape[0]
    shift_x, shift_y = (ny * depth).bit_length() - 1, depth.bit_length() - 1
    lane = lax.broadcasted_iota(jnp.int32, (1, depth), 1)

    @pl.loop(0, total // 8)
    def _(i):
        for j in range(8):
            r = i * 8 + j
            cell = incoming[r]
            safe = jnp.maximum(cell, 0)
            x = lax.shift_right_logical(safe, shift_x)
            y = lax.shift_right_logical(safe, shift_y) & (ny - 1)
            z = jnp.where(cell >= 0, safe & (depth - 1), -1)
            for f in range(2):
                row = v0[f, x, pl.ds(y, 1), :]
                picks[f, pl.ds(r, 1), :] = jnp.where(lane == z, row, 0.0)

    devices = total // cap
    ones = jnp.ones((depth, depth), jnp.float32)
    row_id = lax.broadcasted_iota(jnp.int32, (total, depth), 0)
    lane_id = lax.broadcasted_iota(jnp.int32, (total, depth), 1)
    slot = row_id & (cap - 1)
    spread = jnp.zeros((total, depth), jnp.float32)
    for f in range(2):
        wide = jnp.dot(picks[f], ones, precision=lax.Precision.HIGHEST, preferred_element_type=jnp.float32)
        spread = jnp.where(lane_id == slot + f * cap, wide, spread)
    group = lax.broadcasted_iota(jnp.int32, (devices, total), 1)
    first = lax.broadcasted_iota(jnp.int32, (devices, total), 0) * cap
    member = ((group >= first) & (group < first + cap)).astype(jnp.float32)
    picked_out[...] = jnp.dot(
        member, spread, precision=lax.Precision.HIGHEST, preferred_element_type=jnp.float32
    )

    arrive(3)
    v2_copy = pltpu.make_async_copy(v2, v2_out, out_sem.at[1])
    v2_copy.start()
    for phase in range(4):
        sent(phase)
    s1_copy.wait()
    v2_copy.wait()


def last_kernel(v2, s1, mat, weights, v_out, s_out, zs):
    count, ny, depth = s1.shape[1:]
    x0 = pl.program_id(0) * count
    for slot, (f, which) in enumerate(((2, 1), (0, 0), (1, 0))):
        block = v2[f, pl.ds(x0 + W, count), PAD : PAD + ny, :].reshape(count * ny, depth)
        zs[slot] = depth_product(block, weights[which]).reshape(count, ny, depth)

    @pl.loop(0, count)
    def _(p):
        x = x0 + p
        for f in range(3):
            v_out[f, p] = own(v2, f, x, 0, ny)
        for f, change in enumerate(stress_parts(v2, lambda k: zs[k, p], x, 0, ny, mat[0, p], mat[1, p])):
            s_out[f, p] = s1[f, p] + change


def body(
    velocity, stress, material, src_x, src_y, src_amp, chan_block, chan_cell, chan_azimuth, gauge
):
    nx, ny, depth = material.shape[1:]
    devices = lax.axis_size("gx") * lax.axis_size("gy")
    per_device = chan_cell.shape[0]
    cap = max(2, 2 * per_device // devices)
    target = chan_block[:, 0]
    owners = jnp.arange(devices, dtype=jnp.int32)
    member = (target[:, None] == owners[None, :]).astype(jnp.int32)
    before = jnp.cumsum(member, axis=0) - member
    slot_rank = jnp.sum(before * member, axis=1)
    slot_index = target * cap + slot_rank
    slot_match = (
        slot_index[:, None] == jnp.arange(devices * cap, dtype=jnp.int32)[None, :]
    ).astype(jnp.int32)
    filled = jnp.sum(slot_match, axis=0)
    chosen = jnp.sum(slot_match * chan_cell[:, None], axis=0)
    requests = jnp.where(filled > 0, chosen, -1).reshape(devices, cap)
    incoming = lax.all_to_all(requests, ("gx", "gy"), split_axis=0, concat_axis=0, tiled=True)

    anchor_x, anchor_y = lax.axis_index("gx") * nx, lax.axis_index("gy") * ny
    hit_x = (src_x[:, None, :] - anchor_x == jnp.arange(depth, dtype=jnp.int32)[None, :, None]).astype(jnp.float32)
    hit_y = (src_y[:, None, :] - anchor_y == jnp.arange(ny, dtype=jnp.int32)[None, :, None]).astype(jnp.float32)
    force = jnp.einsum("syk,sxk->syx", hit_y, hit_x * src_amp[:, None, :], precision=lax.Precision.HIGHEST)

    weights = jnp.asarray(depth_weights(depth))
    f32 = jnp.float32
    ext = (nx + 2 * W, ny + 2 * PAD, depth)
    total = devices * cap
    any_space = pl.BlockSpec(memory_space=pl.ANY)
    vmem = pl.BlockSpec(memory_space=pltpu.VMEM)
    s1, v2, picked = pl.pallas_call(
        functools.partial(main_kernel, (nx, ny, depth), cap),
        out_shape=(
            jax.ShapeDtypeStruct((6, nx, ny, depth), f32),
            jax.ShapeDtypeStruct((3,) + ext, f32),
            jax.ShapeDtypeStruct((devices, depth), f32),
        ),
        in_specs=[any_space] * 3 + [vmem, vmem, pl.BlockSpec(memory_space=pltpu.SMEM)],
        out_specs=(any_space, any_space, vmem),
        scratch_shapes=[
            pltpu.VMEM((6,) + ext, f32),
            pltpu.VMEM((6,) + ext, f32),
            pltpu.VMEM((3, nx, ny, depth), f32),
            pltpu.VMEM((3,) + ext, f32),
            pltpu.VMEM((3,) + ext, f32),
            pltpu.VMEM((3, nx, ny, depth), f32),
            pltpu.VMEM((3, nx, ny, depth), f32),
            pltpu.VMEM((2, total, depth), f32),
            pltpu.SemaphoreType.DMA((3,)),
            pltpu.SemaphoreType.DMA((4, 4)),
            pltpu.SemaphoreType.DMA((4, 4)),
            pltpu.SemaphoreType.DMA((2,)),
        ],
        compiler_params=pltpu.CompilerParams(
            collective_id=0, has_side_effects=True, vmem_limit_bytes=52 * 2**20
        ),
        cost_estimate=pl.CostEstimate(flops=2 * 10**9, bytes_accessed=24 * 2**20, transcendentals=0),
        name="steps",
    )(stress, velocity, material, weights, force, incoming.reshape(-1))

    chunk = 4
    velocity_out, stress_out = pl.pallas_call(
        last_kernel,
        grid=(nx // chunk,),
        out_shape=(
            jax.ShapeDtypeStruct((3, nx, ny, depth), f32),
            jax.ShapeDtypeStruct((6, nx, ny, depth), f32),
        ),
        in_specs=[
            pl.BlockSpec((3,) + ext, lambda i: (0, 0, 0, 0), pipeline_mode=pl.Buffered(1)),
            pl.BlockSpec((6, chunk, ny, depth), lambda i: (0, i, 0, 0)),
            pl.BlockSpec((2, chunk, ny, depth), lambda i: (0, i, 0, 0)),
            pl.BlockSpec((2, 2 * depth, 2 * depth), lambda i: (0, 0, 0)),
        ],
        out_specs=(
            pl.BlockSpec((3, chunk, ny, depth), lambda i: (0, i, 0, 0)),
            pl.BlockSpec((6, chunk, ny, depth), lambda i: (0, i, 0, 0)),
        ),
        scratch_shapes=[pltpu.VMEM((3, chunk, ny, depth), f32)],
        compiler_params=pltpu.CompilerParams(vmem_limit_bytes=24 * 2**20),
        cost_estimate=pl.CostEstimate(flops=10**9, bytes_accessed=24 * 2**20, transcendentals=0),
        name="last_stress",
    )(v2, s1, material, weights)

    back = jnp.stack([picked[:, :cap], picked[:, cap : 2 * cap]])
    returned = lax.all_to_all(back, ("gx", "gy"), split_axis=1, concat_axis=1, tiled=True)
    flat_back = returned.reshape(2, total)
    values = jnp.sum(slot_match.astype(f32)[None] * flat_back[:, None, :], axis=2)
    along = jnp.cos(chan_azimuth) * values[0] + jnp.sin(chan_azimuth) * values[1]
    route = [(i + 1, i) for i in range(devices - 1)]
    following = lax.ppermute(along, ("gx", "gy"), route)
    joined = jnp.concatenate([along, following])
    offsets = jnp.arange(per_device, dtype=jnp.int32)[:, None] + gauge[:, None]
    ahead_hit = (offsets == jnp.arange(2 * per_device, dtype=jnp.int32)[None, :]).astype(f32)
    ahead = jnp.sum(ahead_hit * joined[None, :], axis=1)
    strain = (ahead - along) / gauge.astype(f32)
    return velocity_out, stress_out, strain


def solution(mesh):
    grid = P(None, "gx", "gy", None)
    line = P(("gx", "gy"))
    return jax.shard_map(
        body,
        mesh=mesh,
        in_specs=(grid, grid, grid, P(), P(), P(), P(("gx", "gy"), None), line, line, line),
        out_specs=(grid, grid, line),
        check_vma=False,
    )
```

```python
import functools

import jax
import jax.numpy as jnp
import ml_dtypes
import numpy as np
from jax import lax
from jax.experimental import pallas as pl
from jax.experimental.pallas import tpu as pltpu
from jax.sharding import PartitionSpec as P

STEPS = 2
COEFFS = (1225.0 / 1024.0, -245.0 / 3072.0, 49.0 / 5120.0, -5.0 / 7168.0)
DT = 0.2
W = 4
PAD = 8
PLANES = 4
MESH = pl.DeviceIdType.MESH


def depth_weights(depth):
    out = np.zeros((2, 2 * depth, 2 * depth), np.float32)
    for which, shift in ((0, 0), (1, -1)):
        table = np.zeros((depth, depth), np.float64)
        for target in range(depth):
            for order in range(1, 5):
                for source, sign in ((target + shift + order, 1.0), (target + shift + 1 - order, -1.0)):
                    if 0 <= source < depth:
                        table[source, target] += sign * COEFFS[order - 1]
        hi = table.astype(np.float32).astype(ml_dtypes.bfloat16).astype(np.float32)
        lo = (table - hi).astype(np.float32)
        out[which, :depth, :depth] = hi
        out[which, :depth, depth:] = lo
        out[which, depth:, :depth] = hi
    return out.astype(ml_dtypes.bfloat16)


def depth_product(values, weights):
    depth = values.shape[1]
    hi = values.astype(jnp.bfloat16)
    lo = (values - hi.astype(jnp.float32)).astype(jnp.bfloat16)
    both = jnp.concatenate([hi, lo], axis=1)
    out = jnp.dot(both, weights, preferred_element_type=jnp.float32)
    return out[:, :depth] + out[:, depth:]


def weighted(load, forward):
    total = None
    shift = 0 if forward else -1
    for order in range(1, 5):
        term = COEFFS[order - 1] * (load(shift + order) - load(shift + 1 - order))
        total = term if total is None else total + term
    return total


def diff_x(ref, f, x, r0, nr, forward):
    return weighted(lambda k: ref[f, x + (W + k), PAD + r0 : PAD + r0 + nr, :], forward)


def diff_y(ref, f, x, r0, nr, forward):
    return weighted(lambda k: ref[f, x + W, PAD + r0 + k : PAD + r0 + k + nr, :], forward)


def own(ref, f, x, r0, nr):
    return ref[f, x + W, PAD + r0 : PAD + r0 + nr, :]


def stress_parts(v, z_of, x, r0, nr, lam, mu):
    exx = diff_x(v, 0, x, r0, nr, False)
    eyy = diff_y(v, 1, x, r0, nr, False)
    ezz = z_of(0)
    common = (DT * lam) * (exx + eyy + ezz)
    dmu = DT * mu
    dmu2 = 2.0 * dmu
    return (
        common + dmu2 * exx,
        dmu * (z_of(1) + diff_x(v, 2, x, r0, nr, True)),
        dmu * (diff_y(v, 0, x, r0, nr, True) + diff_x(v, 1, x, r0, nr, True)),
        dmu * (z_of(2) + diff_y(v, 2, x, r0, nr, True)),
        common + dmu2 * eyy,
        common + dmu2 * ezz,
    )


def main_kernel(
    sizes, cap, stress, velocity, material, weights, src_x, src_y, src_amp, chan,
    s1_out, v2_out, strain_out,
    s0, s1, v0, v1, v2, mat, zs, picks, force, asked, inc, inc_scalar, reply, back, flat, along_ref, follow,
    load_sem, send_sem, recv_sem, out_sem, ask_send, ask_recv, reply_send, reply_recv, along_sem,
):
    nx, ny, depth = sizes
    gx, gy = lax.axis_index("gx"), lax.axis_index("gy")
    size_y = lax.axis_size("gy")
    last_x, last_y = lax.axis_size("gx") - 1, size_y - 1
    devices = lax.axis_size("gx") * size_y
    me = gx * size_y + gy
    sides = (
        (gx > 0, "gx", gx - 1),
        (gx < last_x, "gx", gx + 1),
        (gy > 0, "gy", gy - 1),
        (gy < last_y, "gy", gy + 1),
    )
    fields_of = {"s": ((0, 3), (2, 5)), "v": ((0, 3), (0, 3))}
    rows = (slice(PAD, PAD + ny),)[0]
    planes = slice(W, W + nx)

    loads = [
        pltpu.make_async_copy(stress, s0.at[:, planes, rows, :], load_sem.at[0]),
        pltpu.make_async_copy(velocity, v0, load_sem.at[1]),
        pltpu.make_async_copy(material, mat, load_sem.at[2]),
    ]
    for copy in loads:
        copy.start()

    for ref, kind in ((s0, "s"), (s1, "s"), (v1, "v"), (v2, "v")):
        (xa, xb), (ya, yb) = fields_of[kind]

        @pl.when(gx == 0)
        def _():
            ref[xa:xb, 0:W] = jnp.zeros((xb - xa, W, ny + 2 * PAD, depth), jnp.float32)

        @pl.when(gx == last_x)
        def _():
            ref[xa:xb, W + nx :] = jnp.zeros((xb - xa, W, ny + 2 * PAD, depth), jnp.float32)

        @pl.when(gy == 0)
        def _():
            @pl.loop(0, nx)
            def _(x):
                ref[ya:yb, x + W, 0:PAD] = jnp.zeros((yb - ya, PAD, depth), jnp.float32)

        @pl.when(gy == last_y)
        def _():
            @pl.loop(0, nx)
            def _(x):
                ref[ya:yb, x + W, PAD + ny :] = jnp.zeros((yb - ya, PAD, depth), jnp.float32)

    def peer(distance):
        other = lax.rem(me + distance + devices, devices)
        return {"gx": lax.div(other, size_y), "gy": lax.rem(other, size_y)}

    barrier = pltpu.get_barrier_semaphore()

    @pl.loop(1, devices)
    def _(d):
        pl.semaphore_signal(barrier, inc=1, device_id=peer(d), device_id_type=MESH)

    pl.semaphore_wait(barrier, devices - 1)

    def ask(d):
        return pltpu.make_async_remote_copy(
            src_ref=asked.at[d], dst_ref=inc.at[d], send_sem=ask_send.at[d], recv_sem=ask_recv.at[d],
            device_id=peer(d), device_id_type=MESH,
        )

    def answer(d):
        return pltpu.make_async_remote_copy(
            src_ref=reply.at[d], dst_ref=back.at[d], send_sem=reply_send.at[d], recv_sem=reply_recv.at[d],
            device_id=peer(-d), device_id_type=MESH,
        )

    pass_on = pltpu.make_async_remote_copy(
        src_ref=along_ref, dst_ref=follow, send_sem=along_sem.at[0], recv_sem=along_sem.at[1],
        device_id=peer(-1), device_id_type=MESH,
    )

    def transfer(phase, kind, source, target, side, from_input):
        (xa, xb), (ya, yb) = fields_of[kind]
        ox, oy = (0, 0) if from_input else (W, PAD)
        all_x, all_y = slice(ox, ox + nx), slice(oy, oy + ny)
        if side == 0:
            src = source.at[xa:xb, ox : ox + W, all_y, :]
            dst = target.at[xa:xb, W + nx : 2 * W + nx, rows, :]
        elif side == 1:
            src = source.at[xa:xb, ox + nx - W : ox + nx, all_y, :]
            dst = target.at[xa:xb, 0:W, rows, :]
        elif side == 2:
            src = source.at[ya:yb, all_x, oy : oy + W, :]
            dst = target.at[ya:yb, planes, PAD + ny : PAD + ny + W, :]
        else:
            src = source.at[ya:yb, all_x, oy + ny - W : oy + ny, :]
            dst = target.at[ya:yb, planes, PAD - W : PAD, :]
        return pltpu.make_async_remote_copy(
            src_ref=src, dst_ref=dst,
            send_sem=send_sem.at[phase, side], recv_sem=recv_sem.at[phase, side],
            device_id={sides[side][1]: sides[side][2]}, device_id_type=MESH,
        )

    plan = (("s", stress, s0, True), ("v", v1, v1, False), ("s", s1, s1, False), ("v", v2, v2, False))

    def send(phase, which):
        kind, source, target, from_input = plan[phase]
        for side in which:
            @pl.when(sides[side][0])
            def _():
                transfer(phase, kind, source, target, side, from_input).start()

    def arrive(phase):
        kind, source, target, from_input = plan[phase]
        for side in range(4):
            @pl.when(sides[side ^ 1][0])
            def _():
                transfer(phase, kind, source, target, side, from_input).wait_recv()

    def sent(phase):
        kind, source, target, from_input = plan[phase]
        for side in range(4):
            @pl.when(sides[side][0])
            def _():
                transfer(phase, kind, source, target, side, from_input).wait_send()

    def depth_pass(ref, jobs):
        @pl.loop(0, nx // PLANES)
        def _(i):
            x = i * PLANES
            for slot, (f, forward) in enumerate(jobs):
                block = ref[f, pl.ds(x + W, PLANES), PAD : PAD + ny, :].reshape(PLANES * ny, depth)
                out = depth_product(block, weights[0 if forward else 1])
                zs[slot, pl.ds(x, PLANES)] = out.reshape(PLANES, ny, depth)

    def velocity_plane(step, s, x, r0, nr):
        old = (lambda f: v0[f, x, r0 : r0 + nr, :]) if step == 0 else (lambda f: own(v1, f, x, r0, nr))
        new = v1 if step == 0 else v2
        z = lambda k: zs[k, x, r0 : r0 + nr, :]
        db = DT * mat[2, x, r0 : r0 + nr, :]

        def put(f, value):
            updated = old(f) + db * value
            new[f, x + W, PAD + r0 : PAD + r0 + nr, :] = updated
            if step == 1 and f < 2:
                v0[f, x, r0 : r0 + nr, :] = updated

        put(0, diff_x(s, 0, x, r0, nr, True) + diff_y(s, 2, x, r0, nr, False) + z(0))
        put(1, diff_x(s, 2, x, r0, nr, False) + diff_y(s, 4, x, r0, nr, True) + z(1))
        load = pltpu.roll(force[step, r0 : r0 + nr, :], depth - x, 1)
        lane = lax.broadcasted_iota(jnp.int32, (nr, depth), 1)
        rate = diff_x(s, 1, x, r0, nr, False) + diff_y(s, 3, x, r0, nr, False) + z(2)
        put(2, rate + jnp.where(lane == 0, load, 0.0))

    def stress_plane(x, r0, nr):
        lam, mu = mat[0, x, r0 : r0 + nr, :], mat[1, x, r0 : r0 + nr, :]
        z = lambda k: zs[k, x, r0 : r0 + nr, :]
        for f, change in enumerate(stress_parts(v1, z, x, r0, nr, lam, mu)):
            s1[f, x + W, PAD + r0 : PAD + r0 + nr, :] = own(s0, f, x, r0, nr) + change

    def interior(update):
        @pl.loop(W, nx - W)
        def _(x):
            update(x, 8, ny - 16)

    def edges_y(update):
        @pl.loop(0, nx)
        def _(x):
            update(x, 0, 8)
            update(x, ny - 8, 8)

    def edges_x(update):
        @pl.loop(0, 2 * W)
        def _(i):
            update(jnp.where(i < W, i, i + nx - 2 * W), 8, ny - 16)

    def update_of(phase):
        if phase == 1:
            return stress_plane
        return functools.partial(velocity_plane, phase // 2, s0 if phase == 0 else s1)

    v_jobs = ((1, False), (3, False), (5, True))
    s_jobs = ((2, False), (0, True), (1, True))
    send(0, (2, 3, 0, 1))

    segment = chan.shape[1]
    exact = lax.Precision.HIGHEST
    f32 = jnp.float32
    rel = chan[0:1, :].astype(jnp.int32) - me
    rel = jnp.where(rel < 0, rel + devices, rel)
    member = (rel == lax.broadcasted_iota(jnp.int32, (devices, segment), 0)).astype(f32)
    earlier = (
        lax.broadcasted_iota(jnp.int32, (segment, segment), 0)
        < lax.broadcasted_iota(jnp.int32, (segment, segment), 1)
    ).astype(f32)
    before = jnp.dot(member, earlier, preferred_element_type=f32)
    rank = jnp.sum(before * member, axis=0, keepdims=True).astype(jnp.int32)
    slots = lax.broadcasted_iota(jnp.int32, (depth, segment), 0)
    requests = lax.dot_general(
        member * (chan[1:2, :] + 1.0), (rank == slots).astype(f32), (((1,), (1,)), ((), ())),
        precision=exact, preferred_element_type=f32,
    )
    requests = (requests + 0.5).astype(jnp.int32) - 1
    for d in range(devices):
        asked[d] = requests[d : d + 1, :]
    inc[0] = requests[0:1, :]

    @pl.loop(1, devices)
    def _(d):
        ask(d).start()

    for step in range(STEPS):
        hit_y = src_y[step : step + 1, :] - gy * ny == lax.broadcasted_iota(jnp.int32, (ny, src_y.shape[1]), 0)
        hit_x = src_x[step : step + 1, :] - gx * nx == lax.broadcasted_iota(jnp.int32, (depth, src_x.shape[1]), 0)
        force[step] = lax.dot_general(
            hit_y.astype(f32), jnp.where(hit_x, src_amp[step : step + 1, :], 0.0), (((1,), (1,)), ((), ())),
            precision=exact, preferred_element_type=f32,
        )

    loads[0].wait()
    for phase, (ref, jobs) in enumerate(((s0, v_jobs), (v1, s_jobs), (s1, v_jobs))):
        update = update_of(phase)
        depth_pass(ref, jobs)
        if phase == 0:
            loads[1].wait()
            loads[2].wait()
        interior(update)
        arrive(phase)
        edges_y(update)
        send(phase + 1, (2, 3))
        edges_x(update)
        send(phase + 1, (0, 1))
        if phase == 1:
            s1_copy = pltpu.make_async_copy(s1.at[:, planes, rows, :], s1_out, out_sem.at[0])
            s1_copy.start()

    total = devices * cap
    shift_x, shift_y = (ny * depth).bit_length() - 1, depth.bit_length() - 1
    lane = lax.broadcasted_iota(jnp.int32, (1, depth), 1)

    @pl.loop(1, devices)
    def _(d):
        ask(d).wait_recv()

    to_scalar = pltpu.make_async_copy(inc, inc_scalar, load_sem.at[3])
    to_scalar.start()
    to_scalar.wait()

    @pl.loop(0, devices)
    def _(d):
        for j in range(cap):
            r = d * cap + j
            cell = inc_scalar[d, 0, j]
            safe = jnp.maximum(cell, 0)
            x = lax.shift_right_logical(safe, shift_x) & (nx - 1)
            y = lax.shift_right_logical(safe, shift_y) & (ny - 1)
            z = jnp.where(cell >= 0, safe & (depth - 1), -1)
            for f in range(2):
                row = v0[f, x, pl.ds(y, 1), :]
                picks[f, pl.ds(r, 1), :] = jnp.where(lane == z, row, 0.0)

    ones = jnp.ones((depth, depth), jnp.float32)
    row_id = lax.broadcasted_iota(jnp.int32, (total, depth), 0)
    lane_id = lax.broadcasted_iota(jnp.int32, (total, depth), 1)
    slot = row_id & (cap - 1)
    spread = jnp.zeros((total, depth), jnp.float32)
    for f in range(2):
        wide = jnp.dot(picks[f], ones, precision=lax.Precision.HIGHEST, preferred_element_type=jnp.float32)
        spread = jnp.where(lane_id == slot + f * cap, wide, spread)
    group = lax.broadcasted_iota(jnp.int32, (devices, total), 1)
    first = lax.broadcasted_iota(jnp.int32, (devices, total), 0) * cap
    member_rows = ((group >= first) & (group < first + cap)).astype(jnp.float32)
    picked = jnp.dot(member_rows, spread, precision=exact, preferred_element_type=f32)
    for d in range(devices):
        reply[d] = picked[d : d + 1, :]
    flat[0:1, :] = picked[0:1, :]

    @pl.loop(1, devices)
    def _(d):
        answer(d).start()

    @pl.loop(1, devices)
    def _(d):
        answer(d).wait_recv()

    for d in range(1, devices):
        flat[d : d + 1, :] = back[d]
    columns = lax.dot_general(
        flat[...], member, (((0,), (0,)), ((), ())), precision=exact, preferred_element_type=f32
    )
    vel_x = jnp.sum(jnp.where(slots == rank, columns, 0.0), axis=0, keepdims=True)
    vel_y = jnp.sum(jnp.where(slots == rank + cap, columns, 0.0), axis=0, keepdims=True)
    along = chan[2:3, :] * vel_x + chan[3:4, :] * vel_y
    along_ref[...] = along

    @pl.when(me > 0)
    def _():
        pass_on.start()

    @pl.when(me == devices - 1)
    def _():
        follow[...] = jnp.zeros(follow.shape, f32)

    @pl.when(me < devices - 1)
    def _():
        pass_on.wait_recv()

    gauge = chan[4:5, :]
    joined = jnp.concatenate([along, follow[...]], axis=1)
    ahead = jnp.zeros((1, segment), f32)
    for g in range(2, 17):
        ahead = jnp.where(gauge == g, joined[:, g : g + segment], ahead)
    strain_out[...] = (ahead - along) / gauge

    arrive(3)
    v2_copy = pltpu.make_async_copy(v2, v2_out, out_sem.at[1])
    v2_copy.start()
    for phase in range(4):
        sent(phase)

    @pl.loop(1, devices)
    def _(d):
        ask(d).wait_send()
        answer(d).wait_send()

    @pl.when(me > 0)
    def _():
        pass_on.wait_send()

    s1_copy.wait()
    v2_copy.wait()


def last_kernel(v2, s1, mat, weights, v_out, s_out, zs):
    count, ny, depth = s1.shape[1:]
    x0 = pl.program_id(0) * count
    for slot, (f, which) in enumerate(((2, 1), (0, 0), (1, 0))):
        block = v2[f, pl.ds(x0 + W, count), PAD : PAD + ny, :].reshape(count * ny, depth)
        zs[slot] = depth_product(block, weights[which]).reshape(count, ny, depth)

    @pl.loop(0, count)
    def _(p):
        x = x0 + p
        for f in range(3):
            v_out[f, p] = own(v2, f, x, 0, ny)
        for f, change in enumerate(stress_parts(v2, lambda k: zs[k, p], x, 0, ny, mat[0, p], mat[1, p])):
            s_out[f, p] = s1[f, p] + change


def body(
    velocity, stress, material, src_x, src_y, src_amp, chan_block, chan_cell, chan_azimuth, gauge
):
    nx, ny, depth = material.shape[1:]
    devices = lax.axis_size("gx") * lax.axis_size("gy")
    per_device = chan_cell.shape[0]
    cap = max(2, 2 * per_device // devices)
    f32 = jnp.float32
    rows = [chan_block[:, 0].astype(f32), chan_cell.astype(f32), jnp.cos(chan_azimuth), jnp.sin(chan_azimuth)]
    chan = jnp.stack(rows + [gauge.astype(f32)] * 4)

    weights = jnp.asarray(depth_weights(depth))
    ext = (nx + 2 * W, ny + 2 * PAD, depth)
    total = devices * cap
    any_space = pl.BlockSpec(memory_space=pl.ANY)
    vmem = pl.BlockSpec(memory_space=pltpu.VMEM)
    s1, v2, strain = pl.pallas_call(
        functools.partial(main_kernel, (nx, ny, depth), cap),
        out_shape=(
            jax.ShapeDtypeStruct((6, nx, ny, depth), f32),
            jax.ShapeDtypeStruct((3,) + ext, f32),
            jax.ShapeDtypeStruct((1, per_device), f32),
        ),
        in_specs=[any_space] * 3 + [vmem] * 5,
        out_specs=(any_space, any_space, vmem),
        scratch_shapes=[
            pltpu.VMEM((6,) + ext, f32),
            pltpu.VMEM((6,) + ext, f32),
            pltpu.VMEM((3, nx, ny, depth), f32),
            pltpu.VMEM((3,) + ext, f32),
            pltpu.VMEM((3,) + ext, f32),
            pltpu.VMEM((3, nx, ny, depth), f32),
            pltpu.VMEM((3, nx, ny, depth), f32),
            pltpu.VMEM((2, total, depth), f32),
            pltpu.VMEM((STEPS, ny, depth), f32),
            pltpu.VMEM((devices, 1, depth), jnp.int32),
            pltpu.VMEM((devices, 1, depth), jnp.int32),
            pltpu.SMEM((devices, 1, depth), jnp.int32),
            pltpu.VMEM((devices, 1, depth), f32),
            pltpu.VMEM((devices, 1, depth), f32),
            pltpu.VMEM((devices, depth), f32),
            pltpu.VMEM((1, per_device), f32),
            pltpu.VMEM((1, per_device), f32),
            pltpu.SemaphoreType.DMA((4,)),
            pltpu.SemaphoreType.DMA((4, 4)),
            pltpu.SemaphoreType.DMA((4, 4)),
            pltpu.SemaphoreType.DMA((2,)),
            pltpu.SemaphoreType.DMA((devices,)),
            pltpu.SemaphoreType.DMA((devices,)),
            pltpu.SemaphoreType.DMA((devices,)),
            pltpu.SemaphoreType.DMA((devices,)),
            pltpu.SemaphoreType.DMA((2,)),
        ],
        compiler_params=pltpu.CompilerParams(
            collective_id=0, has_side_effects=True, vmem_limit_bytes=52 * 2**20
        ),
        cost_estimate=pl.CostEstimate(flops=2 * 10**9, bytes_accessed=24 * 2**20, transcendentals=0),
        name="steps",
    )(stress, velocity, material, weights, src_x, src_y, src_amp, chan)

    chunk = 4
    velocity_out, stress_out = pl.pallas_call(
        last_kernel,
        grid=(nx // chunk,),
        out_shape=(
            jax.ShapeDtypeStruct((3, nx, ny, depth), f32),
            jax.ShapeDtypeStruct((6, nx, ny, depth), f32),
        ),
        in_specs=[
            pl.BlockSpec((3,) + ext, lambda i: (0, 0, 0, 0), pipeline_mode=pl.Buffered(1)),
            pl.BlockSpec((6, chunk, ny, depth), lambda i: (0, i, 0, 0)),
            pl.BlockSpec((2, chunk, ny, depth), lambda i: (0, i, 0, 0)),
            pl.BlockSpec((2, 2 * depth, 2 * depth), lambda i: (0, 0, 0)),
        ],
        out_specs=(
            pl.BlockSpec((3, chunk, ny, depth), lambda i: (0, i, 0, 0)),
            pl.BlockSpec((6, chunk, ny, depth), lambda i: (0, i, 0, 0)),
        ),
        scratch_shapes=[pltpu.VMEM((3, chunk, ny, depth), f32)],
        compiler_params=pltpu.CompilerParams(vmem_limit_bytes=56 * 2**20),
        cost_estimate=pl.CostEstimate(flops=10**9, bytes_accessed=24 * 2**20, transcendentals=0),
        name="last_stress",
    )(v2, s1, material, weights)

    return velocity_out, stress_out, strain.reshape(-1)


def solution(mesh):
    grid = P(None, "gx", "gy", None)
    line = P(("gx", "gy"))
    return jax.shard_map(
        body,
        mesh=mesh,
        in_specs=(grid, grid, grid, P(), P(), P(), P(("gx", "gy"), None), line, line, line),
        out_specs=(grid, grid, line),
        check_vma=False,
    )
```

```python
import functools

import jax
import jax.numpy as jnp
import ml_dtypes
import numpy as np
from jax import lax
from jax.experimental import pallas as pl
from jax.experimental.pallas import tpu as pltpu
from jax.sharding import PartitionSpec as P

STEPS = 2
COEFFS = (1225.0 / 1024.0, -245.0 / 3072.0, 49.0 / 5120.0, -5.0 / 7168.0)
DT = 0.2
W = 4
PAD = 8
PARTS = 4
PLANES = 4
MESH = pl.DeviceIdType.MESH


def depth_weights(depth):
    out = np.zeros((2, 2 * depth, 2 * depth), np.float32)
    for which, shift in ((0, 0), (1, -1)):
        table = np.zeros((depth, depth), np.float64)
        for target in range(depth):
            for order in range(1, 5):
                for source, sign in ((target + shift + order, 1.0), (target + shift + 1 - order, -1.0)):
                    if 0 <= source < depth:
                        table[source, target] += sign * COEFFS[order - 1]
        hi = table.astype(np.float32).astype(ml_dtypes.bfloat16).astype(np.float32)
        lo = (table - hi).astype(np.float32)
        out[which, :depth, :depth] = hi
        out[which, :depth, depth:] = lo
        out[which, depth:, :depth] = hi
    return out.astype(ml_dtypes.bfloat16)


def depth_product(values, weights):
    depth = values.shape[1]
    hi = values.astype(jnp.bfloat16)
    lo = (values - hi.astype(jnp.float32)).astype(jnp.bfloat16)
    both = jnp.concatenate([hi, lo], axis=1)
    out = jnp.dot(both, weights, preferred_element_type=jnp.float32)
    return out[:, :depth] + out[:, depth:]


def weighted(load, forward):
    total = None
    shift = 0 if forward else -1
    for order in range(1, 5):
        term = COEFFS[order - 1] * (load(shift + order) - load(shift + 1 - order))
        total = term if total is None else total + term
    return total


def diff_x(ref, f, x, r0, nr, forward):
    return weighted(lambda k: ref[f, x + (W + k), PAD + r0 : PAD + r0 + nr, :], forward)


def diff_y(ref, f, x, r0, nr, forward):
    return weighted(lambda k: ref[f, x + W, PAD + r0 + k : PAD + r0 + k + nr, :], forward)


def own(ref, f, x, r0, nr):
    return ref[f, x + W, PAD + r0 : PAD + r0 + nr, :]


def stress_parts(v, z_of, x, r0, nr, lam, mu):
    exx = diff_x(v, 0, x, r0, nr, False)
    eyy = diff_y(v, 1, x, r0, nr, False)
    ezz = z_of(0)
    common = (DT * lam) * (exx + eyy + ezz)
    dmu = DT * mu
    dmu2 = 2.0 * dmu
    return (
        common + dmu2 * exx,
        dmu * (z_of(1) + diff_x(v, 2, x, r0, nr, True)),
        dmu * (diff_y(v, 0, x, r0, nr, True) + diff_x(v, 1, x, r0, nr, True)),
        dmu * (z_of(2) + diff_y(v, 2, x, r0, nr, True)),
        common + dmu2 * eyy,
        common + dmu2 * ezz,
    )


def main_kernel(
    sizes, cap, stress, velocity, material, weights_in, src_x_in, src_y_in, src_amp_in,
    block_in, cell_in, azimuth_in, gauge_in,
    v_out, s_out, strain_out,
    s0, s1, v0, v1, v2, mat, zs, picks, force, asked, inc, inc_scalar, reply, back, flat, along_ref, follow,
    weights, src_x, src_y, src_amp, block, cells, azimuth, gauge,
    load_sem, send_sem, recv_sem, y_send, y_recv, out_sem, ask_send, ask_recv, reply_send, reply_recv, along_sem,
):
    nx, ny, depth = sizes
    gx, gy = lax.axis_index("gx"), lax.axis_index("gy")
    size_y = lax.axis_size("gy")
    last_x, last_y = lax.axis_size("gx") - 1, size_y - 1
    devices = lax.axis_size("gx") * size_y
    me = gx * size_y + gy
    sides = (
        (gx > 0, "gx", gx - 1),
        (gx < last_x, "gx", gx + 1),
        (gy > 0, "gy", gy - 1),
        (gy < last_y, "gy", gy + 1),
    )
    fields_of = {"s": ((0, 3), (2, 5)), "v": ((0, 3), (0, 3))}
    groups_of = {"s": ((2, 4, False), (4, 5, True)), "v": ((0, 1, True), (1, 2, False), (2, 3, True))}
    part = nx // PARTS
    rows = (slice(PAD, PAD + ny),)[0]
    planes = slice(W, W + nx)

    loads = [
        pltpu.make_async_copy(stress, s0.at[:, planes, rows, :], load_sem.at[0]),
        pltpu.make_async_copy(velocity, v0, load_sem.at[1]),
        pltpu.make_async_copy(material, mat, load_sem.at[2]),
    ]
    small = (
        (weights_in, weights), (src_x_in, src_x), (src_y_in, src_y), (src_amp_in, src_amp),
        (block_in, block), (cell_in, cells), (azimuth_in, azimuth), (gauge_in, gauge),
    )
    for number, (source, target) in enumerate(small):
        loads.append(pltpu.make_async_copy(source, target, load_sem.at[4 + number]))
    for copy in loads[3:] + loads[:3]:
        copy.start()

    for ref, kind in ((s0, "s"), (s1, "s"), (v1, "v"), (v2, "v")):
        (xa, xb), (ya, yb) = fields_of[kind]

        @pl.when(gx == 0)
        def _():
            ref[xa:xb, 0:W] = jnp.zeros((xb - xa, W, ny + 2 * PAD, depth), jnp.float32)

        @pl.when(gx == last_x)
        def _():
            ref[xa:xb, W + nx :] = jnp.zeros((xb - xa, W, ny + 2 * PAD, depth), jnp.float32)

        @pl.when(gy == 0)
        def _():
            @pl.loop(0, nx)
            def _(x):
                ref[ya:yb, x + W, 0:PAD] = jnp.zeros((yb - ya, PAD, depth), jnp.float32)

        @pl.when(gy == last_y)
        def _():
            @pl.loop(0, nx)
            def _(x):
                ref[ya:yb, x + W, PAD + ny :] = jnp.zeros((yb - ya, PAD, depth), jnp.float32)

    def peer(distance):
        other = lax.rem(me + distance + devices, devices)
        return {"gx": lax.div(other, size_y), "gy": lax.rem(other, size_y)}

    barrier = pltpu.get_barrier_semaphore()

    @pl.loop(1, devices)
    def _(d):
        pl.semaphore_signal(barrier, inc=1, device_id=peer(d), device_id_type=MESH)

    pl.semaphore_wait(barrier, devices - 1)

    def ask(d):
        return pltpu.make_async_remote_copy(
            src_ref=asked.at[d], dst_ref=inc.at[d], send_sem=ask_send.at[d], recv_sem=ask_recv.at[d],
            device_id=peer(d), device_id_type=MESH,
        )

    def answer(d):
        return pltpu.make_async_remote_copy(
            src_ref=reply.at[d], dst_ref=back.at[d], send_sem=reply_send.at[d], recv_sem=reply_recv.at[d],
            device_id=peer(-d), device_id_type=MESH,
        )

    pass_on = pltpu.make_async_remote_copy(
        src_ref=along_ref, dst_ref=follow, send_sem=along_sem.at[0], recv_sem=along_sem.at[1],
        device_id=peer(-1), device_id_type=MESH,
    )

    plan = (("s", stress, s0, True), ("v", v1, v1, False), ("s", s1, s1, False), ("v", v2, v2, False))

    def transfer_x(phase, side):
        kind, source, target, from_input = plan[phase]
        xa, xb = fields_of[kind][0]
        ox, oy = (0, 0) if from_input else (W, PAD)
        start, landing = (ox, W + nx) if side == 0 else (ox + nx - W, 0)
        return pltpu.make_async_remote_copy(
            src_ref=source.at[xa:xb, start : start + W, oy : oy + ny, :],
            dst_ref=target.at[xa:xb, landing : landing + W, rows, :],
            send_sem=send_sem.at[phase, side], recv_sem=recv_sem.at[phase, side],
            device_id={"gx": sides[side][2]}, device_id_type=MESH,
        )

    def transfers_y(phase, side, piece):
        kind, source, target, from_input = plan[phase]
        ox, oy = (0, 0) if from_input else (W, PAD)
        first = piece * part
        out = []
        for number, (ya, yb, forward) in enumerate(groups_of[kind]):
            width = W if forward == (side == 2) else W - 1
            start, landing = (oy, PAD + ny) if side == 2 else (oy + ny - width, PAD - width)
            out.append(pltpu.make_async_remote_copy(
                src_ref=source.at[ya:yb, ox + first : ox + first + part, start : start + width, :],
                dst_ref=target.at[ya:yb, W + first : W + first + part, landing : landing + width, :],
                send_sem=y_send.at[phase, side - 2, piece, number],
                recv_sem=y_recv.at[phase, side - 2, piece, number],
                device_id={"gy": sides[side][2]}, device_id_type=MESH,
            ))
        return out

    def copies(phase, side, piece):
        return [transfer_x(phase, side)] if side < 2 else transfers_y(phase, side, piece)

    def send(phase, which, piece=0):
        for side in which:
            @pl.when(sides[side][0])
            def _():
                for copy in copies(phase, side, piece):
                    copy.start()

    def arrive(phase, which, piece=0):
        for side in which:
            @pl.when(sides[side ^ 1][0])
            def _():
                for copy in copies(phase, side, piece):
                    copy.wait_recv()

    def sent(phase):
        for side in range(4):
            @pl.when(sides[side][0])
            def _():
                for piece in range(PARTS if side > 1 else 1):
                    for copy in copies(phase, side, piece):
                        copy.wait_send()

    def depth_pass(ref, jobs):
        @pl.loop(0, nx // PLANES)
        def _(i):
            x = i * PLANES
            for slot, (f, forward) in enumerate(jobs):
                block = ref[f, pl.ds(x + W, PLANES), PAD : PAD + ny, :].reshape(PLANES * ny, depth)
                out = depth_product(block, weights[0 if forward else 1])
                zs[slot, pl.ds(x, PLANES)] = out.reshape(PLANES, ny, depth)

    def velocity_plane(step, s, x, r0, nr):
        old = (lambda f: v0[f, x, r0 : r0 + nr, :]) if step == 0 else (lambda f: own(v1, f, x, r0, nr))
        new = v1 if step == 0 else v2
        z = lambda k: zs[k, x, r0 : r0 + nr, :]
        db = DT * mat[2, x, r0 : r0 + nr, :]

        def put(f, value):
            updated = old(f) + db * value
            new[f, x + W, PAD + r0 : PAD + r0 + nr, :] = updated
            if step == 1 and f < 2:
                v0[f, x, r0 : r0 + nr, :] = updated

        put(0, diff_x(s, 0, x, r0, nr, True) + diff_y(s, 2, x, r0, nr, False) + z(0))
        put(1, diff_x(s, 2, x, r0, nr, False) + diff_y(s, 4, x, r0, nr, True) + z(1))
        load = pltpu.roll(force[step, r0 : r0 + nr, :], depth - x, 1)
        lane = lax.broadcasted_iota(jnp.int32, (nr, depth), 1)
        rate = diff_x(s, 1, x, r0, nr, False) + diff_y(s, 3, x, r0, nr, False) + z(2)
        put(2, rate + jnp.where(lane == 0, load, 0.0))

    def stress_plane(v, s, new, x, r0, nr):
        lam, mu = mat[0, x, r0 : r0 + nr, :], mat[1, x, r0 : r0 + nr, :]
        z = lambda k: zs[k, x, r0 : r0 + nr, :]
        for f, change in enumerate(stress_parts(v, z, x, r0, nr, lam, mu)):
            new[f, x + W, PAD + r0 : PAD + r0 + nr, :] = own(s, f, x, r0, nr) + change

    def interior(update):
        @pl.loop(W, nx - W)
        def _(x):
            update(x, 8, ny - 16)

    def edges_y(update, piece):
        @pl.loop(piece * part, (piece + 1) * part)
        def _(x):
            update(x, 0, 8)
            update(x, ny - 8, 8)

    def edges_x(update):
        @pl.loop(0, 2 * W)
        def _(i):
            update(jnp.where(i < W, i, i + nx - 2 * W), 8, ny - 16)

    updates = (
        functools.partial(velocity_plane, 0, s0),
        functools.partial(stress_plane, v1, s0, s1),
        functools.partial(velocity_plane, 1, s1),
        functools.partial(stress_plane, v2, s1, s0),
    )

    def all_edges(phase, done=lambda pieces: None):
        update = updates[phase]

        def piece_of(piece):
            arrive(phase, (2, 3), piece)
            edges_y(update, piece)
            if phase < 3:
                send(phase + 1, (2, 3), piece)

        arrive(phase, (0, 1))
        piece_of(0)
        piece_of(PARTS - 1)
        edges_x(update)
        if phase < 3:
            send(phase + 1, (0, 1))
        done((0, PARTS - 1))
        for piece in range(1, PARTS - 1):
            piece_of(piece)
            done((piece,))

    v_jobs = ((1, False), (3, False), (5, True))
    s_jobs = ((2, False), (0, True), (1, True))
    for piece in (0, PARTS - 1):
        send(0, (2, 3), piece)
    send(0, (0, 1))
    for piece in range(1, PARTS - 1):
        send(0, (2, 3), piece)
    for copy in loads[3:]:
        copy.wait()

    segment = block.shape[1]
    exact = lax.Precision.HIGHEST
    f32 = jnp.float32
    rel = block[...] - me
    rel = jnp.where(rel < 0, rel + devices, rel)
    member = (rel == lax.broadcasted_iota(jnp.int32, (devices, segment), 0)).astype(f32)
    earlier = (
        lax.broadcasted_iota(jnp.int32, (segment, segment), 0)
        < lax.broadcasted_iota(jnp.int32, (segment, segment), 1)
    ).astype(f32)
    before = jnp.dot(member, earlier, preferred_element_type=f32)
    rank = jnp.sum(before * member, axis=0, keepdims=True).astype(jnp.int32)
    slots = lax.broadcasted_iota(jnp.int32, (depth, segment), 0)
    requests = lax.dot_general(
        member * (cells[...] + 1).astype(f32), (rank == slots).astype(f32), (((1,), (1,)), ((), ())),
        precision=exact, preferred_element_type=f32,
    )
    requests = (requests + 0.5).astype(jnp.int32) - 1
    for d in range(devices):
        asked[d] = requests[d : d + 1, :]
    inc[0] = requests[0:1, :]

    @pl.loop(1, devices)
    def _(d):
        ask(d).start()

    for step in range(STEPS):
        hit_y = src_y[step : step + 1, :] - gy * ny == lax.broadcasted_iota(jnp.int32, (ny, src_y.shape[1]), 0)
        hit_x = src_x[step : step + 1, :] - gx * nx == lax.broadcasted_iota(jnp.int32, (depth, src_x.shape[1]), 0)
        force[step] = lax.dot_general(
            hit_y.astype(f32), jnp.where(hit_x, src_amp[step : step + 1, :], 0.0), (((1,), (1,)), ((), ())),
            precision=exact, preferred_element_type=f32,
        )

    loads[0].wait()
    for phase, (ref, jobs) in enumerate(((s0, v_jobs), (v1, s_jobs), (s1, v_jobs))):
        depth_pass(ref, jobs)
        if phase == 0:
            loads[1].wait()
            loads[2].wait()
        interior(updates[phase])
        all_edges(phase)
    v_copy = pltpu.make_async_copy(v2.at[:, planes, rows, :], v_out, out_sem.at[PARTS])
    v_copy.start()

    total = devices * cap
    shift_x, shift_y = (ny * depth).bit_length() - 1, depth.bit_length() - 1
    lane = lax.broadcasted_iota(jnp.int32, (1, depth), 1)

    @pl.loop(1, devices)
    def _(d):
        ask(d).wait_recv()

    to_scalar = pltpu.make_async_copy(inc, inc_scalar, load_sem.at[3])
    to_scalar.start()
    to_scalar.wait()

    @pl.loop(0, devices)
    def _(d):
        for j in range(cap):
            r = d * cap + j
            cell = inc_scalar[d, 0, j]
            safe = jnp.maximum(cell, 0)
            x = lax.shift_right_logical(safe, shift_x) & (nx - 1)
            y = lax.shift_right_logical(safe, shift_y) & (ny - 1)
            z = jnp.where(cell >= 0, safe & (depth - 1), -1)
            for f in range(2):
                row = v0[f, x, pl.ds(y, 1), :]
                picks[f, pl.ds(r, 1), :] = jnp.where(lane == z, row, 0.0)

    ones = jnp.ones((depth, depth), jnp.float32)
    row_id = lax.broadcasted_iota(jnp.int32, (total, depth), 0)
    lane_id = lax.broadcasted_iota(jnp.int32, (total, depth), 1)
    slot = row_id & (cap - 1)
    spread = jnp.zeros((total, depth), jnp.float32)
    for f in range(2):
        wide = jnp.dot(picks[f], ones, precision=lax.Precision.HIGHEST, preferred_element_type=jnp.float32)
        spread = jnp.where(lane_id == slot + f * cap, wide, spread)
    group = lax.broadcasted_iota(jnp.int32, (devices, total), 1)
    first = lax.broadcasted_iota(jnp.int32, (devices, total), 0) * cap
    member_rows = ((group >= first) & (group < first + cap)).astype(jnp.float32)
    picked = jnp.dot(member_rows, spread, precision=exact, preferred_element_type=f32)
    for d in range(devices):
        reply[d] = picked[d : d + 1, :]
    flat[0:1, :] = picked[0:1, :]

    @pl.loop(1, devices)
    def _(d):
        answer(d).start()

    depth_pass(v2, s_jobs)
    interior(updates[3])

    @pl.loop(1, devices)
    def _(d):
        answer(d).wait_recv()

    for d in range(1, devices):
        flat[d : d + 1, :] = back[d]
    columns = lax.dot_general(
        flat[...], member, (((0,), (0,)), ((), ())), precision=exact, preferred_element_type=f32
    )
    vel_x = jnp.sum(jnp.where(slots == rank, columns, 0.0), axis=0, keepdims=True)
    vel_y = jnp.sum(jnp.where(slots == rank + cap, columns, 0.0), axis=0, keepdims=True)
    along = jnp.cos(azimuth[...]) * vel_x + jnp.sin(azimuth[...]) * vel_y
    along_ref[...] = along

    @pl.when(me > 0)
    def _():
        pass_on.start()

    @pl.when(me == devices - 1)
    def _():
        follow[...] = jnp.zeros(follow.shape, f32)

    s_copies = [
        pltpu.make_async_copy(
            s0.at[:, W + piece * part : W + (piece + 1) * part, rows, :],
            s_out.at[:, piece * part : (piece + 1) * part], out_sem.at[piece],
        )
        for piece in range(PARTS)
    ]

    def write(pieces):
        for piece in pieces:
            s_copies[piece].start()

    all_edges(3, write)

    @pl.when(me < devices - 1)
    def _():
        pass_on.wait_recv()

    joined = jnp.concatenate([along, follow[...]], axis=1)
    ahead = jnp.zeros((1, segment), f32)
    for g in range(2, 17):
        ahead = jnp.where(gauge[...] == g, joined[:, g : g + segment], ahead)
    strain_out[...] = (ahead - along) / gauge[...].astype(f32)

    for phase in range(4):
        sent(phase)

    @pl.loop(1, devices)
    def _(d):
        ask(d).wait_send()
        answer(d).wait_send()

    @pl.when(me > 0)
    def _():
        pass_on.wait_send()

    v_copy.wait()
    for copy in s_copies:
        copy.wait()


def body(
    velocity, stress, material, src_x, src_y, src_amp, chan_block, chan_cell, chan_azimuth, gauge
):
    nx, ny, depth = material.shape[1:]
    devices = lax.axis_size("gx") * lax.axis_size("gy")
    per_device = chan_cell.shape[0]
    cap = max(2, 2 * per_device // devices)
    f32 = jnp.float32
    weights = jnp.asarray(depth_weights(depth))
    ext = (nx + 2 * W, ny + 2 * PAD, depth)
    total = devices * cap
    any_space = pl.BlockSpec(memory_space=pl.ANY)
    vmem = pl.BlockSpec(memory_space=pltpu.VMEM)
    velocity_out, stress_out, strain = pl.pallas_call(
        functools.partial(main_kernel, (nx, ny, depth), cap),
        out_shape=(
            jax.ShapeDtypeStruct((3, nx, ny, depth), f32),
            jax.ShapeDtypeStruct((6, nx, ny, depth), f32),
            jax.ShapeDtypeStruct((1, per_device), f32),
        ),
        in_specs=[any_space] * 11,
        out_specs=(any_space, any_space, vmem),
        scratch_shapes=[
            pltpu.VMEM((6,) + ext, f32),
            pltpu.VMEM((6,) + ext, f32),
            pltpu.VMEM((3, nx, ny, depth), f32),
            pltpu.VMEM((3,) + ext, f32),
            pltpu.VMEM((3,) + ext, f32),
            pltpu.VMEM((3, nx, ny, depth), f32),
            pltpu.VMEM((3, nx, ny, depth), f32),
            pltpu.VMEM((2, total, depth), f32),
            pltpu.VMEM((STEPS, ny, depth), f32),
            pltpu.VMEM((devices, 1, depth), jnp.int32),
            pltpu.VMEM((devices, 1, depth), jnp.int32),
            pltpu.SMEM((devices, 1, depth), jnp.int32),
            pltpu.VMEM((devices, 1, depth), f32),
            pltpu.VMEM((devices, 1, depth), f32),
            pltpu.VMEM((devices, depth), f32),
            pltpu.VMEM((1, per_device), f32),
            pltpu.VMEM((1, per_device), f32),
            pltpu.VMEM(weights.shape, weights.dtype),
            pltpu.VMEM(src_x.shape, jnp.int32),
            pltpu.VMEM(src_y.shape, jnp.int32),
            pltpu.VMEM(src_amp.shape, f32),
            pltpu.VMEM((1, per_device), jnp.int32),
            pltpu.VMEM((1, per_device), jnp.int32),
            pltpu.VMEM((1, per_device), f32),
            pltpu.VMEM((1, per_device), jnp.int32),
            pltpu.SemaphoreType.DMA((12,)),
            pltpu.SemaphoreType.DMA((4, 2)),
            pltpu.SemaphoreType.DMA((4, 2)),
            pltpu.SemaphoreType.DMA((4, 2, PARTS, 3)),
            pltpu.SemaphoreType.DMA((4, 2, PARTS, 3)),
            pltpu.SemaphoreType.DMA((PARTS + 1,)),
            pltpu.SemaphoreType.DMA((devices,)),
            pltpu.SemaphoreType.DMA((devices,)),
            pltpu.SemaphoreType.DMA((devices,)),
            pltpu.SemaphoreType.DMA((devices,)),
            pltpu.SemaphoreType.DMA((2,)),
        ],
        compiler_params=pltpu.CompilerParams(
            collective_id=0, has_side_effects=True, vmem_limit_bytes=60 * 2**20
        ),
        cost_estimate=pl.CostEstimate(flops=2 * 10**9, bytes_accessed=24 * 2**20, transcendentals=0),
        name="steps",
    )(stress, velocity, material, weights, src_x, src_y, src_amp, *(
        line.reshape(1, per_device) for line in (chan_block, chan_cell, chan_azimuth, gauge)
    ))
    return velocity_out, stress_out, strain.reshape(-1)


def solution(mesh):
    grid = P(None, "gx", "gy", None)
    line = P(("gx", "gy"))
    return jax.shard_map(
        body,
        mesh=mesh,
        in_specs=(grid, grid, grid, P(), P(), P(), P(("gx", "gy"), None), line, line, line),
        out_specs=(grid, grid, line),
        check_vma=False,
    )
```

```python
import functools

import jax
import jax.numpy as jnp
import ml_dtypes
import numpy as np
from jax import lax
from jax.experimental import pallas as pl
from jax.experimental.pallas import tpu as pltpu
from jax.sharding import PartitionSpec as P

STEPS = 2
COEFFS = (1225.0 / 1024.0, -245.0 / 3072.0, 49.0 / 5120.0, -5.0 / 7168.0)
DT = 0.2
W = 4
PAD = 8
PARTS = 4
PLANES = 4
MESH = pl.DeviceIdType.MESH


def depth_weights(depth):
    out = np.zeros((2, 2 * depth, 2 * depth), np.float32)
    for which, shift in ((0, 0), (1, -1)):
        table = np.zeros((depth, depth), np.float64)
        for target in range(depth):
            for order in range(1, 5):
                for source, sign in ((target + shift + order, 1.0), (target + shift + 1 - order, -1.0)):
                    if 0 <= source < depth:
                        table[source, target] += sign * COEFFS[order - 1]
        hi = table.astype(np.float32).astype(ml_dtypes.bfloat16).astype(np.float32)
        lo = (table - hi).astype(np.float32)
        out[which, :depth, :depth] = hi
        out[which, :depth, depth:] = lo
        out[which, depth:, :depth] = hi
    return out.astype(ml_dtypes.bfloat16)


def depth_product(values, weights):
    depth = values.shape[1]
    hi = values.astype(jnp.bfloat16)
    lo = (values - hi.astype(jnp.float32)).astype(jnp.bfloat16)
    both = jnp.concatenate([hi, lo], axis=1)
    out = jnp.dot(both, weights, preferred_element_type=jnp.float32)
    return out[:, :depth] + out[:, depth:]


def weighted(load, forward):
    total = None
    shift = 0 if forward else -1
    for order in range(1, 5):
        term = COEFFS[order - 1] * (load(shift + order) - load(shift + 1 - order))
        total = term if total is None else total + term
    return total


def diff_x(ref, f, x, r0, nr, forward):
    return weighted(lambda k: ref[f, x + (W + k), PAD + r0 : PAD + r0 + nr, :], forward)


def diff_y(ref, f, x, r0, nr, forward):
    return weighted(lambda k: ref[f, x + W, PAD + r0 + k : PAD + r0 + k + nr, :], forward)


def own(ref, f, x, r0, nr):
    return ref[f, x + W, PAD + r0 : PAD + r0 + nr, :]


def stress_parts(v, z_of, x, r0, nr, lam, mu):
    exx = diff_x(v, 0, x, r0, nr, False)
    eyy = diff_y(v, 1, x, r0, nr, False)
    ezz = z_of(0)
    common = (DT * lam) * (exx + eyy + ezz)
    dmu = DT * mu
    dmu2 = 2.0 * dmu
    return (
        common + dmu2 * exx,
        dmu * (z_of(1) + diff_x(v, 2, x, r0, nr, True)),
        dmu * (diff_y(v, 0, x, r0, nr, True) + diff_x(v, 1, x, r0, nr, True)),
        dmu * (z_of(2) + diff_y(v, 2, x, r0, nr, True)),
        common + dmu2 * eyy,
        common + dmu2 * ezz,
    )


def main_kernel(
    sizes, cap, stress, velocity, material, weights_in, src_x_in, src_y_in, src_amp_in,
    block_in, cell_in, azimuth_in, gauge_in,
    v_out, s_out, strain_out,
    s0, s1, v0, v1, v2, mat, zs, picks, force, asked, inc, inc_scalar, reply, back, flat, along_ref, follow,
    weights, src_x, src_y, src_amp, block, cells, azimuth, gauge,
    load_sem, send_sem, recv_sem, y_send, y_recv, ask_send, ask_recv, reply_send, reply_recv, along_sem,
):
    nx, ny, depth = sizes
    gx, gy = lax.axis_index("gx"), lax.axis_index("gy")
    size_y = lax.axis_size("gy")
    last_x, last_y = lax.axis_size("gx") - 1, size_y - 1
    devices = lax.axis_size("gx") * size_y
    me = gx * size_y + gy
    sides = (
        (gx > 0, "gx", gx - 1),
        (gx < last_x, "gx", gx + 1),
        (gy > 0, "gy", gy - 1),
        (gy < last_y, "gy", gy + 1),
    )
    fields_of = {"s": ((0, 3), (2, 5)), "v": ((0, 3), (0, 3))}
    groups_of = {"s": ((2, 4, False), (4, 5, True)), "v": ((0, 1, True), (1, 2, False), (2, 3, True))}
    part = nx // PARTS
    rows = (slice(PAD, PAD + ny),)[0]
    planes = slice(W, W + nx)

    loads = [
        pltpu.make_async_copy(stress, s0.at[:, planes, rows, :], load_sem.at[0]),
        pltpu.make_async_copy(velocity, v0, load_sem.at[1]),
        pltpu.make_async_copy(material, mat, load_sem.at[2]),
    ]
    small = (
        (weights_in, weights), (src_x_in, src_x), (src_y_in, src_y), (src_amp_in, src_amp),
        (block_in, block), (cell_in, cells), (azimuth_in, azimuth), (gauge_in, gauge),
    )
    for number, (source, target) in enumerate(small):
        loads.append(pltpu.make_async_copy(source, target, load_sem.at[4 + number]))
    for copy in loads[3:] + loads[:3]:
        copy.start()

    for ref, kind in ((s0, "s"), (s1, "s"), (v1, "v"), (v2, "v")):
        (xa, xb), (ya, yb) = fields_of[kind]

        @pl.when(gx == 0)
        def _():
            ref[xa:xb, 0:W] = jnp.zeros((xb - xa, W, ny + 2 * PAD, depth), jnp.float32)

        @pl.when(gx == last_x)
        def _():
            ref[xa:xb, W + nx :] = jnp.zeros((xb - xa, W, ny + 2 * PAD, depth), jnp.float32)

        @pl.when(gy == 0)
        def _():
            @pl.loop(0, nx)
            def _(x):
                ref[ya:yb, x + W, 0:PAD] = jnp.zeros((yb - ya, PAD, depth), jnp.float32)

        @pl.when(gy == last_y)
        def _():
            @pl.loop(0, nx)
            def _(x):
                ref[ya:yb, x + W, PAD + ny :] = jnp.zeros((yb - ya, PAD, depth), jnp.float32)

    def peer(distance):
        other = lax.rem(me + distance + devices, devices)
        return {"gx": lax.div(other, size_y), "gy": lax.rem(other, size_y)}

    barrier = pltpu.get_barrier_semaphore()

    @pl.loop(1, devices)
    def _(d):
        pl.semaphore_signal(barrier, inc=1, device_id=peer(d), device_id_type=MESH)

    pl.semaphore_wait(barrier, devices - 1)

    def ask(d):
        return pltpu.make_async_remote_copy(
            src_ref=asked.at[d], dst_ref=inc.at[d], send_sem=ask_send.at[d], recv_sem=ask_recv.at[d],
            device_id=peer(d), device_id_type=MESH,
        )

    def answer(d):
        return pltpu.make_async_remote_copy(
            src_ref=reply.at[d], dst_ref=back.at[d], send_sem=reply_send.at[d], recv_sem=reply_recv.at[d],
            device_id=peer(-d), device_id_type=MESH,
        )

    pass_on = pltpu.make_async_remote_copy(
        src_ref=along_ref, dst_ref=follow, send_sem=along_sem.at[0], recv_sem=along_sem.at[1],
        device_id=peer(-1), device_id_type=MESH,
    )

    plan = (("s", stress, s0, True), ("v", v1, v1, False), ("s", s1, s1, False), ("v", v2, v2, False))

    def transfer_x(phase, side):
        kind, source, target, from_input = plan[phase]
        xa, xb = fields_of[kind][0]
        ox, oy = (0, 0) if from_input else (W, PAD)
        start, landing = (ox, W + nx) if side == 0 else (ox + nx - W, 0)
        return pltpu.make_async_remote_copy(
            src_ref=source.at[xa:xb, start : start + W, oy : oy + ny, :],
            dst_ref=target.at[xa:xb, landing : landing + W, rows, :],
            send_sem=send_sem.at[phase, side], recv_sem=recv_sem.at[phase, side],
            device_id={"gx": sides[side][2]}, device_id_type=MESH,
        )

    def transfers_y(phase, side, piece):
        kind, source, target, from_input = plan[phase]
        ox, oy = (0, 0) if from_input else (W, PAD)
        first = piece * part
        out = []
        for number, (ya, yb, forward) in enumerate(groups_of[kind]):
            width = W if forward == (side == 2) else W - 1
            start, landing = (oy, PAD + ny) if side == 2 else (oy + ny - width, PAD - width)
            out.append(pltpu.make_async_remote_copy(
                src_ref=source.at[ya:yb, ox + first : ox + first + part, start : start + width, :],
                dst_ref=target.at[ya:yb, W + first : W + first + part, landing : landing + width, :],
                send_sem=y_send.at[phase, side - 2, piece, number],
                recv_sem=y_recv.at[phase, side - 2, piece, number],
                device_id={"gy": sides[side][2]}, device_id_type=MESH,
            ))
        return out

    def copies(phase, side, piece):
        return [transfer_x(phase, side)] if side < 2 else transfers_y(phase, side, piece)

    def send(phase, which, piece=0):
        for side in which:
            @pl.when(sides[side][0])
            def _():
                for copy in copies(phase, side, piece):
                    copy.start()

    def arrive(phase, which, piece=0):
        for side in which:
            @pl.when(sides[side ^ 1][0])
            def _():
                for copy in copies(phase, side, piece):
                    copy.wait_recv()

    def sent(phase):
        for side in range(4):
            @pl.when(sides[side][0])
            def _():
                for piece in range(PARTS if side > 1 else 1):
                    for copy in copies(phase, side, piece):
                        copy.wait_send()

    def depth_pass(ref, jobs):
        @pl.loop(0, nx // PLANES)
        def _(i):
            x = i * PLANES
            for slot, (f, forward) in enumerate(jobs):
                block = ref[f, pl.ds(x + W, PLANES), PAD : PAD + ny, :].reshape(PLANES * ny, depth)
                out = depth_product(block, weights[0 if forward else 1])
                zs[slot, pl.ds(x, PLANES)] = out.reshape(PLANES, ny, depth)

    def velocity_plane(step, s, x, r0, nr):
        old = (lambda f: v0[f, x, r0 : r0 + nr, :]) if step == 0 else (lambda f: own(v1, f, x, r0, nr))
        new = v1 if step == 0 else v2
        z = lambda k: zs[k, x, r0 : r0 + nr, :]
        db = DT * mat[2, x, r0 : r0 + nr, :]

        def put(f, value):
            updated = old(f) + db * value
            new[f, x + W, PAD + r0 : PAD + r0 + nr, :] = updated
            if step == 1:
                v_out[f, x, r0 : r0 + nr, :] = updated

        put(0, diff_x(s, 0, x, r0, nr, True) + diff_y(s, 2, x, r0, nr, False) + z(0))
        put(1, diff_x(s, 2, x, r0, nr, False) + diff_y(s, 4, x, r0, nr, True) + z(1))
        load = pltpu.roll(force[step, r0 : r0 + nr, :], depth - x, 1)
        lane = lax.broadcasted_iota(jnp.int32, (nr, depth), 1)
        rate = diff_x(s, 1, x, r0, nr, False) + diff_y(s, 3, x, r0, nr, False) + z(2)
        put(2, rate + jnp.where(lane == 0, load, 0.0))

    def stress_plane(v, s, new, x, r0, nr):
        px, py = (W, PAD) if new is s1 else (0, 0)
        lam, mu = mat[0, x, r0 : r0 + nr, :], mat[1, x, r0 : r0 + nr, :]
        z = lambda k: zs[k, x, r0 : r0 + nr, :]
        for f, change in enumerate(stress_parts(v, z, x, r0, nr, lam, mu)):
            new[f, x + px, py + r0 : py + r0 + nr, :] = own(s, f, x, r0, nr) + change

    def interior(update):
        @pl.loop(W, nx - W)
        def _(x):
            update(x, 8, ny - 16)

    def edges_y(update, piece):
        @pl.loop(piece * part, (piece + 1) * part)
        def _(x):
            update(x, 0, 8)
            update(x, ny - 8, 8)

    def edges_x(update):
        @pl.loop(0, 2 * W)
        def _(i):
            update(jnp.where(i < W, i, i + nx - 2 * W), 8, ny - 16)

    updates = (
        functools.partial(velocity_plane, 0, s0),
        functools.partial(stress_plane, v1, s0, s1),
        functools.partial(velocity_plane, 1, s1),
        functools.partial(stress_plane, v2, s1, s_out),
    )

    def all_edges(phase):
        update = updates[phase]

        def piece_of(piece):
            arrive(phase, (2, 3), piece)
            edges_y(update, piece)
            if phase < 3:
                send(phase + 1, (2, 3), piece)

        arrive(phase, (0, 1))
        piece_of(0)
        piece_of(PARTS - 1)
        edges_x(update)
        if phase < 3:
            send(phase + 1, (0, 1))
        for piece in range(1, PARTS - 1):
            piece_of(piece)

    v_jobs = ((1, False), (3, False), (5, True))
    s_jobs = ((2, False), (0, True), (1, True))
    for piece in (0, PARTS - 1):
        send(0, (2, 3), piece)
    send(0, (0, 1))
    for piece in range(1, PARTS - 1):
        send(0, (2, 3), piece)
    for copy in loads[3:]:
        copy.wait()

    segment = block.shape[1]
    exact = lax.Precision.HIGHEST
    f32 = jnp.float32
    rel = block[...] - me
    rel = jnp.where(rel < 0, rel + devices, rel)
    member = (rel == lax.broadcasted_iota(jnp.int32, (devices, segment), 0)).astype(f32)
    earlier = (
        lax.broadcasted_iota(jnp.int32, (segment, segment), 0)
        < lax.broadcasted_iota(jnp.int32, (segment, segment), 1)
    ).astype(f32)
    before = jnp.dot(member, earlier, preferred_element_type=f32)
    rank = jnp.sum(before * member, axis=0, keepdims=True).astype(jnp.int32)
    slots = lax.broadcasted_iota(jnp.int32, (depth, segment), 0)
    requests = lax.dot_general(
        member * (cells[...] + 1).astype(f32), (rank == slots).astype(f32), (((1,), (1,)), ((), ())),
        precision=exact, preferred_element_type=f32,
    )
    requests = (requests + 0.5).astype(jnp.int32) - 1
    for d in range(devices):
        asked[d] = requests[d : d + 1, :]
    inc[0] = requests[0:1, :]

    @pl.loop(1, devices)
    def _(d):
        ask(d).start()

    for step in range(STEPS):
        hit_y = src_y[step : step + 1, :] - gy * ny == lax.broadcasted_iota(jnp.int32, (ny, src_y.shape[1]), 0)
        hit_x = src_x[step : step + 1, :] - gx * nx == lax.broadcasted_iota(jnp.int32, (depth, src_x.shape[1]), 0)
        force[step] = lax.dot_general(
            hit_y.astype(f32), jnp.where(hit_x, src_amp[step : step + 1, :], 0.0), (((1,), (1,)), ((), ())),
            precision=exact, preferred_element_type=f32,
        )

    loads[0].wait()
    for phase, (ref, jobs) in enumerate(((s0, v_jobs), (v1, s_jobs), (s1, v_jobs))):
        depth_pass(ref, jobs)
        if phase == 0:
            loads[1].wait()
            loads[2].wait()
        interior(updates[phase])
        all_edges(phase)
    total = devices * cap
    shift_x, shift_y = (ny * depth).bit_length() - 1, depth.bit_length() - 1
    lane = lax.broadcasted_iota(jnp.int32, (1, depth), 1)

    @pl.loop(1, devices)
    def _(d):
        ask(d).wait_recv()

    to_scalar = pltpu.make_async_copy(inc, inc_scalar, load_sem.at[3])
    to_scalar.start()
    to_scalar.wait()

    @pl.loop(0, devices)
    def _(d):
        for j in range(cap):
            r = d * cap + j
            cell = inc_scalar[d, 0, j]
            safe = jnp.maximum(cell, 0)
            x = lax.shift_right_logical(safe, shift_x) & (nx - 1)
            y = lax.shift_right_logical(safe, shift_y) & (ny - 1)
            z = jnp.where(cell >= 0, safe & (depth - 1), -1)
            for f in range(2):
                row = v_out[f, x, pl.ds(y, 1), :]
                picks[f, pl.ds(r, 1), :] = jnp.where(lane == z, row, 0.0)

    ones = jnp.ones((depth, depth), jnp.float32)
    row_id = lax.broadcasted_iota(jnp.int32, (total, depth), 0)
    lane_id = lax.broadcasted_iota(jnp.int32, (total, depth), 1)
    slot = row_id & (cap - 1)
    spread = jnp.zeros((total, depth), jnp.float32)
    for f in range(2):
        wide = jnp.dot(picks[f], ones, precision=lax.Precision.HIGHEST, preferred_element_type=jnp.float32)
        spread = jnp.where(lane_id == slot + f * cap, wide, spread)
    group = lax.broadcasted_iota(jnp.int32, (devices, total), 1)
    first = lax.broadcasted_iota(jnp.int32, (devices, total), 0) * cap
    member_rows = ((group >= first) & (group < first + cap)).astype(jnp.float32)
    picked = jnp.dot(member_rows, spread, precision=exact, preferred_element_type=f32)
    for d in range(devices):
        reply[d] = picked[d : d + 1, :]
    flat[0:1, :] = picked[0:1, :]

    @pl.loop(1, devices)
    def _(d):
        answer(d).start()

    depth_pass(v2, s_jobs)
    interior(updates[3])

    @pl.loop(1, devices)
    def _(d):
        answer(d).wait_recv()

    for d in range(1, devices):
        flat[d : d + 1, :] = back[d]
    columns = lax.dot_general(
        flat[...], member, (((0,), (0,)), ((), ())), precision=exact, preferred_element_type=f32
    )
    vel_x = jnp.sum(jnp.where(slots == rank, columns, 0.0), axis=0, keepdims=True)
    vel_y = jnp.sum(jnp.where(slots == rank + cap, columns, 0.0), axis=0, keepdims=True)
    along = jnp.cos(azimuth[...]) * vel_x + jnp.sin(azimuth[...]) * vel_y
    along_ref[...] = along

    @pl.when(me > 0)
    def _():
        pass_on.start()

    @pl.when(me == devices - 1)
    def _():
        follow[...] = jnp.zeros(follow.shape, f32)

    all_edges(3)

    @pl.when(me < devices - 1)
    def _():
        pass_on.wait_recv()

    joined = jnp.concatenate([along, follow[...]], axis=1)
    ahead = jnp.zeros((1, segment), f32)
    for g in range(2, 17):
        ahead = jnp.where(gauge[...] == g, joined[:, g : g + segment], ahead)
    strain_out[...] = (ahead - along) / gauge[...].astype(f32)

    for phase in range(4):
        sent(phase)

    @pl.loop(1, devices)
    def _(d):
        ask(d).wait_send()
        answer(d).wait_send()

    @pl.when(me > 0)
    def _():
        pass_on.wait_send()


def body(
    velocity, stress, material, src_x, src_y, src_amp, chan_block, chan_cell, chan_azimuth, gauge
):
    nx, ny, depth = material.shape[1:]
    devices = lax.axis_size("gx") * lax.axis_size("gy")
    per_device = chan_cell.shape[0]
    cap = max(2, 2 * per_device // devices)
    f32 = jnp.float32
    weights = jnp.asarray(depth_weights(depth))
    ext = (nx + 2 * W, ny + 2 * PAD, depth)
    total = devices * cap
    any_space = pl.BlockSpec(memory_space=pl.ANY)
    vmem = pl.BlockSpec(memory_space=pltpu.VMEM)
    velocity_out, stress_out, strain = pl.pallas_call(
        functools.partial(main_kernel, (nx, ny, depth), cap),
        out_shape=(
            pltpu.VMEM((3, nx, ny, depth), f32),
            pltpu.VMEM((6, nx, ny, depth), f32),
            jax.ShapeDtypeStruct((1, per_device), f32),
        ),
        in_specs=[any_space] * 11,
        out_specs=(vmem, vmem, vmem),
        scratch_shapes=[
            pltpu.VMEM((6,) + ext, f32),
            pltpu.VMEM((6,) + ext, f32),
            pltpu.VMEM((3, nx, ny, depth), f32),
            pltpu.VMEM((3,) + ext, f32),
            pltpu.VMEM((3,) + ext, f32),
            pltpu.VMEM((3, nx, ny, depth), f32),
            pltpu.VMEM((3, nx, ny, depth), f32),
            pltpu.VMEM((2, total, depth), f32),
            pltpu.VMEM((STEPS, ny, depth), f32),
            pltpu.VMEM((devices, 1, depth), jnp.int32),
            pltpu.VMEM((devices, 1, depth), jnp.int32),
            pltpu.SMEM((devices, 1, depth), jnp.int32),
            pltpu.VMEM((devices, 1, depth), f32),
            pltpu.VMEM((devices, 1, depth), f32),
            pltpu.VMEM((devices, depth), f32),
            pltpu.VMEM((1, per_device), f32),
            pltpu.VMEM((1, per_device), f32),
            pltpu.VMEM(weights.shape, weights.dtype),
            pltpu.VMEM(src_x.shape, jnp.int32),
            pltpu.VMEM(src_y.shape, jnp.int32),
            pltpu.VMEM(src_amp.shape, f32),
            pltpu.VMEM((1, per_device), jnp.int32),
            pltpu.VMEM((1, per_device), jnp.int32),
            pltpu.VMEM((1, per_device), f32),
            pltpu.VMEM((1, per_device), jnp.int32),
            pltpu.SemaphoreType.DMA((12,)),
            pltpu.SemaphoreType.DMA((4, 2)),
            pltpu.SemaphoreType.DMA((4, 2)),
            pltpu.SemaphoreType.DMA((4, 2, PARTS, 3)),
            pltpu.SemaphoreType.DMA((4, 2, PARTS, 3)),
            pltpu.SemaphoreType.DMA((devices,)),
            pltpu.SemaphoreType.DMA((devices,)),
            pltpu.SemaphoreType.DMA((devices,)),
            pltpu.SemaphoreType.DMA((devices,)),
            pltpu.SemaphoreType.DMA((2,)),
        ],
        compiler_params=pltpu.CompilerParams(
            collective_id=0, has_side_effects=True, vmem_limit_bytes=54 * 2**20
        ),
        cost_estimate=pl.CostEstimate(flops=2 * 10**9, bytes_accessed=24 * 2**20, transcendentals=0),
        name="steps",
    )(stress, velocity, material, weights, src_x, src_y, src_amp, *(
        line.reshape(1, per_device) for line in (chan_block, chan_cell, chan_azimuth, gauge)
    ))
    return velocity_out, stress_out, strain.reshape(-1)


def solution(mesh):
    grid = P(None, "gx", "gy", None)
    line = P(("gx", "gy"))
    return jax.shard_map(
        body,
        mesh=mesh,
        in_specs=(grid, grid, grid, P(), P(), P(), P(("gx", "gy"), None), line, line, line),
        out_specs=(grid, grid, line),
        check_vma=False,
    )
```
